32 devices in a mesh: sky: 4 (over y, x), epoch: 8 (over z, core).
Axes of the slice: x: 2, y: 2, z: 4, core: 2. Of those that a mesh axis runs over, the one named last changes fastest.
Arguments:
- params: bfloat16 [512, 64], P('sky'), may hold values from -6 to 6
- basis: bfloat16 [64, 4096], replicated, may hold values from -0.75 to 0.75
- psf_taps: float32 [8, 2, 51], P('epoch'), may hold values from 0.02 to 1
- send_index: int32 [4, 4, 16], P('sky'), may hold values from 0 to 127
- tile_count: int32 [4, 4], P('sky'), may hold values from 0 to 16, as said below
- stamp_row: int32 [4, 4, 16], P('sky'), may hold values from 0 to 256
- stamp_col: int32 [4, 4, 16], P('sky'), may hold values from 0 to 448
- observed: float32 [8, 1024, 512], P('epoch', 'sky'), may hold values from 0 to 6
- background: float32 [8, 1024, 512], P('epoch', 'sky'), may hold values from 0.5 to 2
Outputs:
- param_grad: float32 [512, 64], P('sky')
- residual: float32 [8, 1024, 512], P('epoch', 'sky')
The draws below stay inside these ranges and needn't reach their ends.
Inputs may be any that keep to these rules, and one draw needn't show every extreme that they name: `send_index`: slots with k >= tile_count[t, o] are dead and may name any row; they still lie within range. `tile_count`: some tiles are crowded and receive nearly 16 slots from every owner; in every draw at least one tile receives exactly 16 from owner 0. `stamp_row`: A stamp lies inside its tile's canvas.
All inputs are finite; a program needn't handle non-finite values.
Results may differ from the reference program's by a relative error of at most 0.0003.
Values may be sent and summed in bfloat16 or wider, within the bound.
A program may use at most 64 MiB of HBM per device.

```python
import math
import jax
import jax.numpy as jnp
from jax import lax

P_SIZE = 64
STAMP = 64
TAPS = 51
TR = 256
TW = 512
SRC_DEV = 128
CAP = 16
MARGIN = 32
CANVAS = 320
NROWS = 1024
SOURCES = 512
N_SKY = 4
N_EPOCH = 8


def draw_tile_count(key, part):
    key_one, key_two, key_three, key_four = jax.random.split(jax.random.fold_in(key, 17), 4)
    crowded = jax.random.randint(key_one, (N_SKY,), 0, 4) == 0
    chosen = jax.random.randint(key_two, (), 0, N_SKY)
    crowded = crowded | (jnp.arange(N_SKY) == chosen)
    light = jax.random.randint(key_three, (N_SKY, N_SKY), 0, CAP // 2 + 1)
    heavy = CAP - jax.random.randint(key_four, (N_SKY, N_SKY), 0, CAP // 4 + 1)
    count = jnp.where(crowded[:, None], heavy, light)
    first_owner = jnp.arange(N_SKY)[None, :] == 0
    count = jnp.where(crowded[:, None] & first_owner, CAP, count)
    return count.astype(jnp.int32)


def plant(drawn, rng, least, high):
    spot = [jax.random.randint(jax.random.fold_in(rng, axis), (), 0, length) for axis, length in enumerate(drawn.shape)]
    main_axis = drawn.shape.index(max(drawn.shape))
    next_to = spot[:main_axis] + [(spot[main_axis] + 1) % drawn.shape[main_axis]] + spot[main_axis + 1:]
    return drawn.at[tuple(spot)].set(least).at[tuple(next_to)].set(high)


def block_scale(key, extent, cuts, least, top_value):
    def one(position, blocks):
        steps = jax.random.uniform(jax.random.fold_in(jax.random.fold_in(key, 6), position), (blocks,), jnp.float32, least / len(cuts), top_value / len(cuts))
        return jnp.repeat(jnp.exp(steps), extent[position] // blocks).reshape((-1,) + (1,) * (len(extent) - position - 1))

    loudness = one(*cuts[0])
    for cut in cuts[1:]:
        loudness = loudness * one(*cut)
    return loudness


def centred(rng, dims, deviation, most, pieces=(), kind=jnp.bfloat16):
    drawn = jax.random.normal(rng, dims, jnp.float32) * deviation
    if len(pieces) > 0:
        drawn = block_scale(rng, dims, pieces, -0.22, 0.18) * drawn
    return jnp.clip(drawn, min=-most, max=most).astype(kind)


def setup_inputs(seed: int = 0) -> dict:
    streams_of = jax.random.split(jax.random.key(seed), 10)
    return {
        "params": centred(streams_of[0], (SOURCES, P_SIZE), 1.0, 6.0, ((0, 4),)),
        "basis": centred(streams_of[1], (P_SIZE, STAMP * STAMP), P_SIZE ** -0.5, 0.75),
        "psf_taps": jnp.clip(jnp.exp(math.log(1.0) - 3.912023 * jax.random.uniform(streams_of[2], (N_EPOCH, 2, TAPS), jnp.float32) ** block_scale(streams_of[2], (N_EPOCH, 2, TAPS), ((0, 8),), -0.2, 0.2)), 0.02, 1.0),
        "send_index": plant(jax.random.randint(streams_of[3], (N_SKY, N_SKY, CAP), 0, SRC_DEV), jax.random.fold_in(streams_of[3], 1), 0, SRC_DEV - 1).astype(jnp.int32),
        "tile_count": draw_tile_count(jax.random.fold_in(streams_of[9], 71), 0),
        "stamp_row": plant(jax.random.randint(streams_of[5], (N_SKY, N_SKY, CAP), 0, CANVAS - STAMP + 1), jax.random.fold_in(streams_of[5], 1), 0, CANVAS - STAMP).astype(jnp.int32),
        "stamp_col": plant(jax.random.randint(streams_of[6], (N_SKY, N_SKY, CAP), 0, TW - STAMP + 1), jax.random.fold_in(streams_of[6], 1), 0, TW - STAMP).astype(jnp.int32),
        "observed": jnp.clip(6.0 * jax.random.uniform(streams_of[7], (N_EPOCH, NROWS, TW), jnp.float32) ** block_scale(streams_of[7], (N_EPOCH, NROWS, TW), ((0, 8), (1, 4)), -0.2, 0.2), 0.0, 6.0),
        "background": jnp.clip(jnp.exp(math.log(2.0) - 1.3862944 * jax.random.uniform(streams_of[8], (N_EPOCH, NROWS, TW), jnp.float32) ** block_scale(streams_of[8], (N_EPOCH, NROWS, TW), ((0, 8), (1, 4)), -0.2, 0.2)), 0.5, 2.0),
    }


def toeplitz(taps, width):
    half = (taps.shape[0] - 1) // 2
    rows_at = jnp.arange(width, dtype=jnp.int32)[:, None]
    cols_at = jnp.arange(width, dtype=jnp.int32)[None, :]
    where_at = rows_at - cols_at + half
    inside = (where_at >= 0) & (where_at < taps.shape[0])
    return jnp.where(inside, taps[jnp.clip(where_at, 0, taps.shape[0] - 1)], jnp.zeros((), taps.dtype))


def reference(params, basis, psf_taps, send_index, tile_count, stamp_row, stamp_col, observed, background):
    highest = lax.Precision.HIGHEST
    owners = jnp.arange(N_SKY, dtype=jnp.int32)
    global_rows = send_index + (owners * SRC_DEV)[:, None, None]
    dest_rows = jnp.transpose(global_rows, (1, 0, 2)).reshape(N_SKY, -1)
    slot_params = params[dest_rows]
    live = (jnp.arange(CAP, dtype=jnp.int32)[None, None, :] < tile_count[:, :, None]).astype(jnp.float32)
    live = live.reshape(N_SKY, -1)
    intrinsic = jnp.dot(slot_params.reshape(-1, P_SIZE), basis, preferred_element_type=jnp.float32)
    intrinsic = intrinsic.reshape(N_SKY, -1, STAMP, STAMP)
    taps = psf_taps / jnp.sum(psf_taps, axis=-1, keepdims=True)
    row_pos = stamp_row.reshape(N_SKY, -1)
    col_pos = stamp_col.reshape(N_SKY, -1)
    stamp_span = jnp.arange(STAMP, dtype=jnp.int32)
    basis_wide = basis.astype(jnp.float32).T

    def exposure(total, inputs):
        taps_e, obs_e, back_e = inputs
        row_kernel = toeplitz(taps_e[0], STAMP)
        col_kernel = toeplitz(taps_e[1], STAMP)

        def indices(rows_t, cols_t):
            count = rows_t.shape[0]
            rows_full = jnp.broadcast_to(rows_t[:, None, None] + stamp_span[None, :, None], (count, STAMP, STAMP))
            cols_full = jnp.broadcast_to(cols_t[:, None, None] + stamp_span[None, None, :], (count, STAMP, STAMP))
            return rows_full, cols_full

        def render_tile(args):
            intr_t, live_t, rows_t, cols_t = args
            rendered = jnp.einsum('ab,nbc,dc->nad', row_kernel, intr_t, col_kernel, precision=highest)
            rendered = rendered * live_t[:, None, None]
            stamps = lax.optimization_barrier(rendered.astype(jnp.bfloat16)).astype(jnp.float32)
            rows_full, cols_full = indices(rows_t, cols_t)
            return jnp.zeros((CANVAS, TW), jnp.float32).at[rows_full, cols_full].add(stamps)

        canvas = lax.map(render_tile, (intrinsic, live, row_pos, col_pos))
        core = canvas[:, MARGIN:MARGIN + TR]
        below = jnp.concatenate([jnp.zeros((1, MARGIN, TW), jnp.float32), canvas[:-1, MARGIN + TR:]], axis=0)
        above = jnp.concatenate([canvas[1:, :MARGIN], jnp.zeros((1, MARGIN, TW), jnp.float32)], axis=0)
        core = core.at[:, :MARGIN].add(below).at[:, TR - MARGIN:].add(above)
        image = core.reshape(NROWS, TW)
        model = back_e + jax.nn.softplus(image)
        residual = (obs_e / model - 1.0) * jax.nn.sigmoid(image)
        padded = jnp.pad(residual.astype(jnp.bfloat16), ((MARGIN, MARGIN), (0, 0)))

        def adjoint_tile(args):
            tile, live_t, rows_t, cols_t = args
            reach = lax.dynamic_slice_in_dim(padded, (tile * TR).astype(jnp.int32), CANVAS, 0)
            rows_full, cols_full = indices(rows_t, cols_t)
            window = reach[rows_full, cols_full].astype(jnp.float32)
            pulled = jnp.einsum('ba,nbc,cd->nad', row_kernel, window, col_kernel, precision=highest)
            pulled = pulled * live_t[:, None, None]
            return jnp.dot(pulled.reshape(-1, STAMP * STAMP), basis_wide, precision=highest)

        grads = lax.map(adjoint_tile, (owners, live, row_pos, col_pos))
        return total + grads, residual

    start = jnp.zeros((N_SKY, N_SKY * CAP, P_SIZE), jnp.float32)
    total, residual = lax.scan(exposure, start, (taps, observed, background))
    param_grad = jnp.zeros((SOURCES, P_SIZE), jnp.float32).at[dest_rows.reshape(-1)].add(total.reshape(-1, P_SIZE))
    return param_grad, residual
```

```python
import functools

import jax
import jax.numpy as jnp
from jax import lax
from jax.experimental import pallas as pl
from jax.experimental.pallas import tpu as pltpu
from jax.sharding import PartitionSpec as P

MESH = pl.DeviceIdType.MESH
LANES = 128


def split_two(value):
    high = value.astype(jnp.bfloat16)
    return high, (value - high.astype(jnp.float32)).astype(jnp.bfloat16)


def wide_dot(left, right, dims=(((1,), (0,)), ((), ()))):
    return lax.dot_general(left, right, dims, preferred_element_type=jnp.float32)


def kernel(
    n_sky,
    n_epoch,
    params,
    basis,
    taps_scalar,
    taps_vector,
    send_index,
    tile_count,
    stamp_row,
    stamp_col,
    observed,
    background,
    grad_out,
    residual_out,
    outgoing,
    incoming,
    observed_halo,
    background_halo,
    basis_rows,
    basis_mixed,
    rendered_rows,
    rendered,
    stamps,
    row_one,
    moved,
    canvas,
    light_halo,
    reach,
    window_rows,
    windows,
    slot_grad,
    reduce_in,
    piece,
    gather_in,
    param_send,
    param_recv,
    halo_send,
    halo_recv,
    light_send,
    light_recv,
    reduce_send,
    reduce_recv,
    gather_send,
    gather_recv,
):
    me_s = lax.axis_index("sky")
    me_e = lax.axis_index("epoch")
    n_par = params.shape[1]
    size = 64
    half = size // 2
    capacity = send_index.shape[2]
    slots = n_sky * capacity
    tile_rows = observed.shape[1]
    width = observed.shape[2]
    margin = half
    canvas_rows = tile_rows + 2 * margin
    planes = width // LANES
    pairs = size * size // LANES
    per = slots // n_epoch
    ratio = capacity // per
    n_taps = taps_vector.shape[2]
    reach_taps = (n_taps - 1) // 2
    my_owner = me_e // ratio
    has_above = me_s > 0
    has_below = me_s < n_sky - 1

    barrier = pltpu.get_barrier_semaphore()
    for step in range(1, n_sky):
        pl.semaphore_signal(
            barrier, 1, device_id=(lax.rem(me_s + step, n_sky), me_e), device_id_type=MESH
        )
    for step in range(1, n_epoch):
        pl.semaphore_signal(
            barrier, 1, device_id=(me_s, lax.rem(me_e + step, n_epoch)), device_id_type=MESH
        )
    for tile in range(n_sky):
        for part in range(ratio):
            sender = me_s * ratio + part

            @pl.when(jnp.logical_not((me_s == tile) & (sender == me_e)))
            def _():
                pl.semaphore_signal(barrier, 1, device_id=(tile, sender), device_id_type=MESH)

    slot_at = lax.broadcasted_iota(jnp.int32, (slots, params.shape[0]), 0)
    source_at = lax.broadcasted_iota(jnp.int32, (slots, params.shape[0]), 1)
    named = jnp.zeros_like(slot_at)
    for tile in range(n_sky):
        for k in range(capacity):
            named = jnp.where(slot_at == tile * capacity + k, send_index[0, tile, k], named)
    picked = wide_dot((named == source_at).astype(jnp.bfloat16), params[...]).astype(jnp.bfloat16)
    for tile in range(n_sky):
        outgoing[tile] = picked[tile * capacity : (tile + 1) * capacity]
    incoming[me_s] = outgoing[me_s]

    pl.semaphore_wait(
        barrier,
        (n_sky - 1) + (n_epoch - 1) + n_epoch - jnp.where(my_owner == me_s, 1, 0),
    )

    def param_copy(step):
        other = lax.rem(me_s + step, n_sky)
        return pltpu.make_async_remote_copy(
            src_ref=outgoing.at[other],
            dst_ref=incoming.at[me_s],
            send_sem=param_send.at[step],
            recv_sem=param_recv.at[step],
            device_id=(other, me_e),
            device_id_type=MESH,
        )

    def halo_copies(upward):
        other = me_s - 1 if upward else me_s + 1
        start = 0 if upward else tile_rows - margin
        slot = 1 if upward else 0
        return [
            pltpu.make_async_remote_copy(
                src_ref=array.at[0, pl.ds(start, margin)],
                dst_ref=landing.at[slot],
                send_sem=halo_send.at[which, slot],
                recv_sem=halo_recv.at[which, slot],
                device_id=(other, me_e),
                device_id_type=MESH,
            )
            for which, (array, landing) in enumerate(
                ((observed, observed_halo), (background, background_halo))
            )
        ]

    def light_copy(upward):
        other = me_s - 1 if upward else me_s + 1
        start = 0 if upward else canvas_rows - 2 * margin
        slot = 1 if upward else 0
        return pltpu.make_async_remote_copy(
            src_ref=canvas.at[pl.ds(start, 2 * margin)],
            dst_ref=light_halo.at[slot],
            send_sem=light_send.at[slot],
            recv_sem=light_recv.at[slot],
            device_id=(other, me_e),
            device_id_type=MESH,
        )

    for step in range(1, n_sky):
        param_copy(step).start()

    @pl.when(has_above)
    def _():
        for copy in halo_copies(True):
            copy.start()

    @pl.when(has_below)
    def _():
        for copy in halo_copies(False):
            copy.start()

    @pl.when(jnp.logical_not(has_above))
    def _():
        light_halo[0] = jnp.zeros(light_halo.shape[1:], jnp.float32)
        observed_halo[0] = jnp.zeros(observed_halo.shape[1:], jnp.float32)
        background_halo[0] = jnp.ones(background_halo.shape[1:], jnp.float32)

    @pl.when(jnp.logical_not(has_below))
    def _():
        light_halo[1] = jnp.zeros(light_halo.shape[1:], jnp.float32)
        observed_halo[1] = jnp.zeros(observed_halo.shape[1:], jnp.float32)
        background_halo[1] = jnp.ones(background_halo.shape[1:], jnp.float32)

    def natural(value):
        return 2 * (value % half) + value // half

    row_a = natural(lax.broadcasted_iota(jnp.int32, (size, size), 0))
    row_b = natural(lax.broadcasted_iota(jnp.int32, (size, size), 1))
    row_where = row_a - row_b + reach_taps
    col_c = lax.broadcasted_iota(jnp.int32, (LANES, LANES), 0)
    col_d = lax.broadcasted_iota(jnp.int32, (LANES, LANES), 1)
    col_where = jnp.where(
        col_c // size == col_d // size, col_d % size - col_c % size + reach_taps, -1
    )

    def tap_step(tap, both):
        row_k, col_k = both
        return (
            jnp.where(row_where == tap, taps_scalar[0, 0, tap], row_k),
            jnp.where(col_where == tap, taps_scalar[0, 1, tap], col_k),
        )

    row_k, col_k = lax.fori_loop(
        0,
        n_taps,
        tap_step,
        (jnp.zeros((size, size), jnp.float32), jnp.zeros((LANES, LANES), jnp.float32)),
        unroll=3,
    )
    total = jnp.sum(taps_vector[0], axis=1, keepdims=True)
    row_high, row_low = split_two(row_k / total[0:1])
    col_high, col_low = split_two(col_k / total[1:2])

    lane_half = lax.broadcasted_iota(jnp.int32, (half, LANES), 1) < size
    for pair in range(pairs):
        basis_rows[pl.ds(pair * n_par, n_par), :] = basis[
            :, pair * LANES : (pair + 1) * LANES
        ].astype(jnp.float32)

    def swapped(one, two):
        return (
            jnp.where(lane_half, one, pltpu.roll(two, size, 1)),
            jnp.where(lane_half, pltpu.roll(one, size, 1), two),
        )

    group = 8

    def mix_group(index, carry):
        for inner in range(group):
            pp = index * group + inner
            one = basis_rows[pl.ds(2 * pp, half, stride=n_par), :]
            two = basis_rows[pl.ds(2 * pp + 1, half, stride=n_par), :]
            first, second = swapped(one, two)
            lanes = pl.ds(inner * LANES, LANES)
            basis_mixed[:half, lanes] = first.astype(jnp.bfloat16)
            basis_mixed[half:, lanes] = second.astype(jnp.bfloat16)
        mixed = basis_mixed[...]
        by_row = wide_dot(row_high, mixed) + wide_dot(row_low, mixed)
        tall = jnp.concatenate(
            [by_row[:, inner * LANES : (inner + 1) * LANES] for inner in range(group)], axis=0
        )
        high, low = split_two(tall)
        done = wide_dot(high, col_high) + (wide_dot(low, col_high) + wide_dot(high, col_low))
        for inner in range(group):
            pp = index * group + inner
            base = inner * size
            first, second = swapped(done[base : base + half], done[base + half : base + size])
            rendered_rows[pl.ds(2 * pp, half, stride=n_par), :] = first
            rendered_rows[pl.ds(2 * pp + 1, half, stride=n_par), :] = second
        return carry

    lax.fori_loop(0, n_par // 2 // group, mix_group, 0)
    for pair in range(pairs):
        high, low = split_two(rendered_rows[pl.ds(pair * n_par, n_par), :])
        rendered[:n_par, pair * LANES : (pair + 1) * LANES] = high
        rendered[n_par:, pair * LANES : (pair + 1) * LANES] = low

    for step in range(1, n_sky):
        copy = param_copy(step)
        copy.wait()
    par_slot = lax.broadcasted_iota(jnp.int32, (slots, n_par), 0)
    live = jnp.zeros((slots, n_par), jnp.float32)
    for owner in range(n_sky):
        inside = (par_slot >= owner * capacity) & (
            par_slot < owner * capacity + tile_count[0, owner]
        )
        live = jnp.where(inside & (par_slot < (owner + 1) * capacity), 1.0, live)
    here = incoming[...].reshape(slots, n_par).astype(jnp.float32)
    here = jnp.where(live > 0, here, 0.0).astype(jnp.bfloat16)
    wide = 8
    for block in range(pairs // wide):
        lanes = slice(block * wide * LANES, (block + 1) * wide * LANES)
        made = wide_dot(here, rendered[:n_par, lanes]) + wide_dot(here, rendered[n_par:, lanes])
        for inner in range(wide):
            stamps[pl.ds((block * wide + inner) * slots, slots), :] = made[
                :, inner * LANES : (inner + 1) * LANES
            ]

    lane_row = lax.broadcasted_iota(jnp.int32, (1, LANES), 1)
    level = lax.broadcasted_iota(jnp.int32, (canvas_rows, LANES), 0)
    offset = level - natural(lax.broadcasted_iota(jnp.int32, (canvas_rows, LANES), 1) % size)
    canvas[...] = jnp.zeros_like(canvas)

    def place_owner(owner, carry):
        def place_pair(pair, inner_carry):
            rows = []
            for which in range(2):
                k = 2 * pair + which
                col = stamp_col[0, owner, k]
                rows.append(stamp_row[0, owner, k])
                stamp = stamps[pl.ds(owner * capacity + k, half, stride=slots), :]
                shift = lax.rem(col, LANES)
                even = pltpu.roll(stamp, shift, 1)
                odd = pltpu.roll(even, size, 1)
                for plane in range(planes):
                    at = lane_row + (plane * LANES) - col
                    inside = (at >= 0) & (at < size)
                    for parity, data in enumerate((even, odd)):
                        start = pl.multiple_of(k * size + parity * half, half)
                        moved[pl.ds(start, half), plane * LANES : (plane + 1) * LANES] = jnp.where(
                            inside, data, 0.0
                        ).astype(jnp.bfloat16)
            target = jnp.where(lane_row < size, rows[0], rows[1])
            lanes = pl.ds(pl.multiple_of(pair * LANES, LANES), LANES)
            row_one[:, lanes] = jnp.where(offset == target, 1.0, 0.0).astype(jnp.bfloat16)
            return inner_carry

        lax.fori_loop(0, capacity // 2, place_pair, 0, unroll=2)
        canvas[...] += wide_dot(row_one[...], moved[...])
        return carry

    lax.fori_loop(0, n_sky, place_owner, 0)

    @pl.when(has_above)
    def _():
        light_copy(True).start()

    @pl.when(has_below)
    def _():
        light_copy(False).start()

    def residual_of(image, seen, sky):
        decay = jnp.exp(-jnp.abs(image))
        model = sky + (jnp.maximum(image, 0.0) + jnp.log(1.0 + decay))
        numerator = jnp.where(image >= 0, 1.0, decay)
        return (seen - model) * numerator / (model * (1.0 + decay))

    def keep(value, start):
        rounded = value.astype(jnp.bfloat16).astype(jnp.float32)
        for plane in range(planes):
            reach[pl.ds(plane * canvas_rows + start, margin), :] = rounded[
                :, plane * LANES : (plane + 1) * LANES
            ]

    def core_chunk(index, carry):
        start = pl.multiple_of(index * margin, margin)
        inner = pl.multiple_of(start - margin, margin)
        value = residual_of(
            canvas[pl.ds(start, margin), :],
            observed[0, pl.ds(inner, margin), :],
            background[0, pl.ds(inner, margin), :],
        )
        residual_out[0, pl.ds(inner, margin), :] = value
        keep(value, start)
        return carry

    chunks = canvas_rows // margin
    lax.fori_loop(2, chunks - 2, core_chunk, 0)
    reach[planes * canvas_rows :, :] = jnp.zeros((canvas_rows, LANES), jnp.float32)

    @pl.when(has_above)
    def _():
        light_copy(True).wait_send()
        light_copy(False).wait_recv()
        for copy in halo_copies(True):
            copy.wait_send()
        for copy in halo_copies(False):
            copy.wait_recv()

    @pl.when(has_below)
    def _():
        light_copy(False).wait_send()
        light_copy(True).wait_recv()
        for copy in halo_copies(False):
            copy.wait_send()
        for copy in halo_copies(True):
            copy.wait_recv()

    for slot, exists in ((0, has_above), (1, has_below)):
        outer = 0 if slot == 0 else canvas_rows - margin
        inner = margin if slot == 0 else canvas_rows - 2 * margin
        outer_light = 0 if slot == 0 else margin
        inner_light = margin - outer_light
        value = residual_of(
            canvas[pl.ds(outer, margin), :] + light_halo[slot, pl.ds(outer_light, margin), :],
            observed_halo[slot],
            background_halo[slot],
        )
        keep(jnp.where(exists, value, 0.0), outer)
        value = residual_of(
            canvas[pl.ds(inner, margin), :] + light_halo[slot, pl.ds(inner_light, margin), :],
            observed[0, pl.ds(inner - margin, margin), :],
            background[0, pl.ds(inner - margin, margin), :],
        )
        residual_out[0, pl.ds(inner - margin, margin), :] = value
        keep(value, inner)

    def pick_owner(owner, carry):
        def pick(k, inner_carry):
            col = stamp_col[0, owner, k]
            row = stamp_row[0, owner, k]
            shift = lax.rem(col, LANES)
            first = (col // LANES) * canvas_rows + row
            back = lax.rem(LANES - shift, LANES)
            halves = []
            for parity in range(2):
                near = reach[pl.ds(first + parity, half, stride=2), :]
                far = reach[pl.ds(first + canvas_rows + parity, half, stride=2), :]
                halves.append(jnp.where(lane_row >= shift, near, far))
            even = pltpu.roll(halves[0], back, 1)
            odd = pltpu.roll(pltpu.roll(halves[1], back, 1), size, 1)
            window_rows[pl.ds(owner * capacity + k, half, stride=slots), :] = jnp.where(
                lane_half, even, odd
            )
            return inner_carry

        return lax.fori_loop(0, capacity, pick, carry, unroll=4)

    lax.fori_loop(0, n_sky, pick_owner, 0)
    for pair in range(pairs):
        windows[:, pair * LANES : (pair + 1) * LANES] = window_rows[
            pl.ds(pair * slots, slots), :
        ].astype(jnp.bfloat16)
    both = wide_dot(windows[...], rendered[...], (((1,), (1,)), ((), ())))
    slot_grad[...] = jnp.where(live > 0, both[:, :n_par] + both[:, n_par:], 0.0)

    def reduce_copy(step):
        other = lax.rem(me_e + step, n_epoch)
        return pltpu.make_async_remote_copy(
            src_ref=slot_grad.at[pl.ds(pl.multiple_of(other * per, per), per)],
            dst_ref=reduce_in.at[step],
            send_sem=reduce_send.at[step],
            recv_sem=reduce_recv.at[step],
            device_id=(me_s, other),
            device_id_type=MESH,
        )

    for step in range(1, n_epoch):
        reduce_copy(step).start()
    summed = slot_grad[pl.ds(pl.multiple_of(me_e * per, per), per), :]
    for step in range(1, n_epoch):
        reduce_copy(step).wait_recv()
        summed = summed + reduce_in[step]
    piece[...] = summed
    my_place = me_s * ratio + lax.rem(me_e, ratio)

    def gather_copy(step):
        return pltpu.make_async_remote_copy(
            src_ref=piece,
            dst_ref=gather_in.at[my_place],
            send_sem=gather_send.at[step],
            recv_sem=gather_recv.at[my_place],
            device_id=(my_owner, lax.rem(me_e + step, n_epoch)),
            device_id_type=MESH,
        )

    for step in range(1, n_epoch):
        gather_copy(step).start()

    @pl.when(my_owner == me_s)
    def _():
        gather_in[my_place] = piece[...]

    @pl.when(my_owner != me_s)
    def _():
        gather_copy(0).start()

    out_source = lax.broadcasted_iota(jnp.int32, (params.shape[0], slots), 0)
    out_slot = lax.broadcasted_iota(jnp.int32, (1, slots), 1)
    out_named = jnp.zeros((1, slots), jnp.int32)
    for tile in range(n_sky):
        for k in range(capacity):
            out_named = jnp.where(
                out_slot == tile * capacity + k, send_index[0, tile, k], out_named
            )
    table = (out_source == out_named).astype(jnp.float32)

    for step in range(1, n_epoch):
        reduce_copy(step).wait_send()
        gather_copy(step).wait_send()

    @pl.when(my_owner != me_s)
    def _():
        gather_copy(0).wait_send()

    for tile in range(n_sky):
        for part in range(ratio):

            @pl.when(jnp.logical_not((me_s == tile) & (me_s * ratio + part == me_e)))
            def _():
                place = tile * ratio + part
                pltpu.make_async_remote_copy(
                    src_ref=piece,
                    dst_ref=gather_in.at[place],
                    send_sem=gather_send.at[0],
                    recv_sem=gather_recv.at[place],
                    device_id=(tile, me_s * ratio + part),
                    device_id_type=MESH,
                ).wait_recv()

    back = gather_in[...].reshape(slots, n_par)
    grad_out[...] = lax.dot_general(
        table,
        back,
        (((1,), (0,)), ((), ())),
        precision=lax.Precision.HIGHEST,
        preferred_element_type=jnp.float32,
    )


def on_device(
    n_sky,
    n_epoch,
    params,
    basis,
    psf_taps,
    send_index,
    tile_count,
    stamp_row,
    stamp_col,
    observed,
    background,
):
    n_par, pixels = basis.shape
    capacity = send_index.shape[2]
    slots = n_sky * capacity
    tile_rows, width = observed.shape[1:]
    size = 64
    margin = size // 2
    canvas_rows = tile_rows + 2 * margin
    planes = width // LANES
    pairs = pixels // LANES
    per = slots // n_epoch
    ratio = capacity // per
    f32, bf16 = jnp.float32, jnp.bfloat16
    vmem = pl.BlockSpec(memory_space=pltpu.VMEM)
    smem = pl.BlockSpec(memory_space=pltpu.SMEM)
    dma = pltpu.SemaphoreType.DMA
    return pl.pallas_call(
        functools.partial(kernel, n_sky, n_epoch),
        out_shape=(
            jax.ShapeDtypeStruct((params.shape[0], n_par), f32),
            jax.ShapeDtypeStruct(observed.shape, f32),
        ),
        in_specs=[vmem, vmem, smem, vmem, smem, smem, smem, smem, vmem, vmem],
        out_specs=(vmem, vmem),
        scratch_shapes=[
            pltpu.VMEM((n_sky, capacity, n_par), bf16),
            pltpu.VMEM((n_sky, capacity, n_par), bf16),
            pltpu.VMEM((2, margin, width), f32),
            pltpu.VMEM((2, margin, width), f32),
            pltpu.VMEM((pairs * n_par, LANES), f32),
            pltpu.VMEM((size, 8 * LANES), bf16),
            pltpu.VMEM((pairs * n_par, LANES), f32),
            pltpu.VMEM((2 * n_par, pixels), bf16),
            pltpu.VMEM((pairs * slots, LANES), f32),
            pltpu.VMEM((canvas_rows, capacity * size), bf16),
            pltpu.VMEM((capacity * size, width), bf16),
            pltpu.VMEM((canvas_rows, width), f32),
            pltpu.VMEM((2, 2 * margin, width), f32),
            pltpu.VMEM(((planes + 1) * canvas_rows, LANES), f32),
            pltpu.VMEM((pairs * slots, LANES), f32),
            pltpu.VMEM((slots, pixels), bf16),
            pltpu.VMEM((slots, n_par), f32),
            pltpu.VMEM((n_epoch, per, n_par), f32),
            pltpu.VMEM((per, n_par), f32),
            pltpu.VMEM((n_sky * ratio, per, n_par), f32),
            dma((n_sky,)),
            dma((n_sky,)),
            dma((2, 2)),
            dma((2, 2)),
            dma((2,)),
            dma((2,)),
            dma((n_epoch,)),
            dma((n_epoch,)),
            dma((n_epoch,)),
            dma((n_sky * ratio,)),
        ],
        compiler_params=pltpu.CompilerParams(
            collective_id=0, has_side_effects=True, vmem_limit_bytes=48 * 1024 * 1024
        ),
    )(
        params,
        basis,
        psf_taps,
        psf_taps,
        send_index,
        tile_count,
        stamp_row,
        stamp_col,
        observed,
        background,
    )


def solution(mesh):
    in_specs = (
        P("sky", None),
        P(),
        P("epoch", None, None),
        P("sky", None, None),
        P("sky", None),
        P("sky", None, None),
        P("sky", None, None),
        P("epoch", "sky", None),
        P("epoch", "sky", None),
    )
    out_specs = (P("sky", None), P("epoch", "sky", None))
    return jax.shard_map(
        functools.partial(on_device, mesh.shape["sky"], mesh.shape["epoch"]),
        mesh=mesh,
        in_specs=in_specs,
        out_specs=out_specs,
        check_vma=False,
    )
```

```python
import functools

import jax
import jax.numpy as jnp
from jax import lax
from jax.experimental import pallas as pl
from jax.experimental.pallas import tpu as pltpu
from jax.sharding import PartitionSpec as P

MESH = pl.DeviceIdType.MESH
LANES = 128


def split_two(value):
    high = value.astype(jnp.bfloat16)
    return high, (value - high.astype(jnp.float32)).astype(jnp.bfloat16)


def wrapped(value, count):
    return jnp.where(value >= count, value - count, value)


def wide_dot(left, right, dims=(((1,), (0,)), ((), ()))):
    return lax.dot_general(left, right, dims, preferred_element_type=jnp.float32)


def kernel(
    n_sky,
    n_epoch,
    params,
    basis,
    taps_scalar,
    taps_vector,
    send_index,
    tile_count,
    stamp_row,
    stamp_col,
    observed,
    background,
    grad_out,
    residual_out,
    outgoing,
    incoming,
    observed_halo,
    background_halo,
    basis_here,
    observed_here,
    background_here,
    basis_rows,
    basis_mixed,
    rendered_rows,
    rendered,
    stamps,
    row_one,
    moved,
    edges,
    middle,
    light_halo,
    reach,
    windows,
    slot_grad,
    reduce_in,
    piece,
    gather_in,
    load_sem,
    param_send,
    param_recv,
    halo_send,
    halo_recv,
    light_send,
    light_recv,
    reduce_send,
    reduce_recv,
    gather_send,
    gather_recv,
):
    me_s = lax.axis_index("sky")
    me_e = lax.axis_index("epoch")
    n_par, n_source = params.shape
    size = 64
    half = size // 2
    capacity = send_index.shape[2]
    slots = n_sky * capacity
    tile_rows = observed.shape[1]
    width = observed.shape[2]
    margin = half
    canvas_rows = tile_rows + 2 * margin
    planes = width // LANES
    pairs = size * size // LANES
    per = slots // n_epoch
    ratio = capacity // per
    n_taps = taps_vector.shape[2]
    reach_taps = (n_taps - 1) // 2
    my_owner = me_e // ratio
    slot_pitch = slots + 8
    par_pitch = n_par + 8
    has_above = me_s > 0
    has_below = me_s < n_sky - 1

    loads = [
        pltpu.make_async_copy(
            basis.at[pl.ds(part * (n_par // 4), n_par // 4)],
            basis_here.at[pl.ds(part * (n_par // 4), n_par // 4)],
            load_sem.at[part],
        )
        for part in range(4)
    ] + [
        pltpu.make_async_copy(observed.at[0], observed_here, load_sem.at[4]),
        pltpu.make_async_copy(background.at[0], background_here, load_sem.at[5]),
    ]
    for load in loads:
        load.start()

    barrier = pltpu.get_barrier_semaphore()
    for step in range(1, n_sky):
        pl.semaphore_signal(
            barrier, 1, device_id=(wrapped(me_s + step, n_sky), me_e), device_id_type=MESH
        )
    for step in range(1, n_epoch):
        pl.semaphore_signal(
            barrier, 1, device_id=(me_s, wrapped(me_e + step, n_epoch)), device_id_type=MESH
        )
    for tile in range(n_sky):
        for part in range(ratio):
            sender = me_s * ratio + part

            @pl.when(jnp.logical_not((me_s == tile) & (sender == me_e)))
            def _():
                pl.semaphore_signal(barrier, 1, device_id=(tile, sender), device_id_type=MESH)

    slot_at = lax.broadcasted_iota(jnp.int32, (8, n_source), 0)
    source_at = lax.broadcasted_iota(jnp.int32, (8, n_source), 1)
    rows_of = []
    for base in range(0, slots, 8):
        named = jnp.zeros_like(slot_at)
        for inner in range(8):
            tile, k = divmod(base + inner, capacity)
            named = jnp.where(slot_at == inner, send_index[0, tile, k], named)
        rows_of.append(jnp.where(named == source_at, 1.0, 0.0))
    table = jnp.concatenate(rows_of, axis=0)
    picked = wide_dot(
        table.astype(jnp.bfloat16), params[...], (((1,), (1,)), ((), ()))
    ).astype(jnp.bfloat16)
    for tile in range(n_sky):
        outgoing[tile] = picked[tile * capacity : (tile + 1) * capacity]
    incoming[me_s] = outgoing[me_s]

    def param_copy(step):
        other = wrapped(me_s + step, n_sky)
        return pltpu.make_async_remote_copy(
            src_ref=outgoing.at[other],
            dst_ref=incoming.at[me_s],
            send_sem=param_send.at[step],
            recv_sem=param_recv.at[step],
            device_id=(other, me_e),
            device_id_type=MESH,
        )

    def halo_copies(upward):
        other = me_s - 1 if upward else me_s + 1
        start = 0 if upward else tile_rows - margin
        slot = 1 if upward else 0
        return [
            pltpu.make_async_remote_copy(
                src_ref=array.at[0, pl.ds(start, margin)],
                dst_ref=landing.at[slot],
                send_sem=halo_send.at[which, slot],
                recv_sem=halo_recv.at[which, slot],
                device_id=(other, me_e),
                device_id_type=MESH,
            )
            for which, (array, landing) in enumerate(
                ((observed, observed_halo), (background, background_halo))
            )
        ]

    def light_copy(upward):
        other = me_s - 1 if upward else me_s + 1
        start = 0 if upward else 2 * margin
        slot = 1 if upward else 0
        return pltpu.make_async_remote_copy(
            src_ref=edges.at[pl.ds(start, 2 * margin)],
            dst_ref=light_halo.at[slot],
            send_sem=light_send.at[slot],
            recv_sem=light_recv.at[slot],
            device_id=(other, me_e),
            device_id_type=MESH,
        )

    @pl.when(jnp.logical_not(has_above))
    def _():
        light_halo[0] = jnp.zeros(light_halo.shape[1:], jnp.float32)
        observed_halo[0] = jnp.zeros(observed_halo.shape[1:], jnp.float32)
        background_halo[0] = jnp.ones(background_halo.shape[1:], jnp.float32)

    @pl.when(jnp.logical_not(has_below))
    def _():
        light_halo[1] = jnp.zeros(light_halo.shape[1:], jnp.float32)
        observed_halo[1] = jnp.zeros(observed_halo.shape[1:], jnp.float32)
        background_halo[1] = jnp.ones(background_halo.shape[1:], jnp.float32)

    def natural(value):
        return 2 * (value & (half - 1)) + (value >> 5)

    row_a = natural(lax.broadcasted_iota(jnp.int32, (size, size), 0))
    row_b = natural(lax.broadcasted_iota(jnp.int32, (size, size), 1))
    row_where = row_a - row_b + reach_taps
    col_c = lax.broadcasted_iota(jnp.int32, (LANES, LANES), 0)
    col_d = lax.broadcasted_iota(jnp.int32, (LANES, LANES), 1)
    col_where = jnp.where(
        (col_c >> 6) == (col_d >> 6),
        (col_d & (size - 1)) - (col_c & (size - 1)) + reach_taps,
        -1,
    )

    def tap_step(tap, both):
        row_k, col_k = both
        return (
            jnp.where(row_where == tap, taps_scalar[0, 0, tap], row_k),
            jnp.where(col_where == tap, taps_scalar[0, 1, tap], col_k),
        )

    row_k, col_k = lax.fori_loop(
        0,
        n_taps,
        tap_step,
        (jnp.zeros((size, size), jnp.float32), jnp.zeros((LANES, LANES), jnp.float32)),
        unroll=3,
    )
    total = jnp.sum(taps_vector[0], axis=1, keepdims=True)
    row_high, row_low = split_two(row_k / total[0:1])
    col_high, col_low = split_two(col_k / total[1:2])
    row_both = jnp.concatenate([row_high, row_low], axis=0)
    col_both = jnp.concatenate(
        [
            jnp.concatenate([col_high, col_low], axis=1),
            jnp.concatenate([col_high, jnp.zeros_like(col_low)], axis=1),
        ],
        axis=0,
    )

    pl.semaphore_wait(
        barrier,
        (n_sky - 1) + (n_epoch - 1) + n_epoch - jnp.where(my_owner == me_s, 1, 0),
    )

    for step in range(1, n_sky):
        param_copy(step).start()

    @pl.when(has_above)
    def _():
        for copy in halo_copies(True):
            copy.start()

    @pl.when(has_below)
    def _():
        for copy in halo_copies(False):
            copy.start()

    for load in loads[:4]:
        load.wait()
    lane_half = lax.broadcasted_iota(jnp.int32, (half, LANES), 1) < size
    for pair in range(pairs):
        basis_rows[pl.ds(pair * par_pitch, n_par), :] = basis_here[
            :, pair * LANES : (pair + 1) * LANES
        ].astype(jnp.float32)

    def swapped(one, two):
        return (
            jnp.where(lane_half, one, pltpu.roll(two, size, 1)),
            jnp.where(lane_half, pltpu.roll(one, size, 1), two),
        )

    group = 8

    def mix_group(index, carry):
        for inner in range(group):
            pp = index * group + inner
            one = basis_rows[pl.ds(2 * pp, half, stride=par_pitch), :]
            two = basis_rows[pl.ds(2 * pp + 1, half, stride=par_pitch), :]
            first, second = swapped(one, two)
            lanes = pl.ds(inner * LANES, LANES)
            basis_mixed[:half, lanes] = first.astype(jnp.bfloat16)
            basis_mixed[half:, lanes] = second.astype(jnp.bfloat16)
        mixed = basis_mixed[...]
        by_row = wide_dot(row_both, mixed)
        by_row = by_row[:size] + by_row[size:]
        tall = jnp.concatenate(
            [by_row[:, inner * LANES : (inner + 1) * LANES] for inner in range(group)], axis=0
        )
        high, low = split_two(tall)
        done = wide_dot(jnp.concatenate([high, low], axis=1), col_both)
        done = done[:, :LANES] + done[:, LANES:]
        for inner in range(group):
            pp = index * group + inner
            base = inner * size
            first, second = swapped(done[base : base + half], done[base + half : base + size])
            rendered_rows[pl.ds(2 * pp, half, stride=par_pitch), :] = first
            rendered_rows[pl.ds(2 * pp + 1, half, stride=par_pitch), :] = second
        return carry

    lax.fori_loop(0, n_par // 2 // group, mix_group, 0)
    for pair in range(pairs):
        high, low = split_two(rendered_rows[pl.ds(pair * par_pitch, n_par), :])
        rendered[:n_par, pair * LANES : (pair + 1) * LANES] = high
        rendered[n_par:, pair * LANES : (pair + 1) * LANES] = low

    for step in range(1, n_sky):
        copy = param_copy(step)
        copy.wait()
    par_slot = lax.broadcasted_iota(jnp.int32, (slots, n_par), 0)
    live = jnp.zeros((slots, n_par), jnp.float32)
    for owner in range(n_sky):
        inside = (par_slot >= owner * capacity) & (
            par_slot < owner * capacity + tile_count[0, owner]
        )
        live = jnp.where(inside & (par_slot < (owner + 1) * capacity), 1.0, live)
    here = incoming[...].reshape(slots, n_par).astype(jnp.float32)
    here = jnp.where(live > 0, here, 0.0)
    here = jnp.concatenate([here, here], axis=1).astype(jnp.bfloat16)
    wide = 8
    for block in range(pairs // wide):
        lanes = slice(block * wide * LANES, (block + 1) * wide * LANES)
        made = wide_dot(here, rendered[:, lanes])
        for inner in range(wide):
            stamps[pl.ds((block * wide + inner) * slot_pitch, slots), :] = made[
                :, inner * LANES : (inner + 1) * LANES
            ]

    lane_row = lax.broadcasted_iota(jnp.int32, (1, LANES), 1)
    level = lax.broadcasted_iota(jnp.int32, (canvas_rows, LANES), 0)
    level = jnp.where(
        level < 2 * margin,
        level,
        jnp.where(level < 4 * margin, level + (canvas_rows - 4 * margin), level - 2 * margin),
    )
    offset = level - natural(lane_row & (size - 1))
    span = capacity * size

    def place_owner(owner, carry):
        base = pl.multiple_of(owner * span, span)
        for pair in range(capacity // 2):
            rows = []
            for which in range(2):
                k = 2 * pair + which
                col = stamp_col[0, owner, k]
                rows.append(stamp_row[0, owner, k])
                stamp = stamps[pl.ds(owner * capacity + k, half, stride=slot_pitch), :]
                even = pltpu.roll(stamp, col & (LANES - 1), 1)
                odd = pltpu.roll(even, size, 1)
                for plane in range(planes):
                    at = lane_row + (plane * LANES) - col
                    inside = (at >= 0) & (at < size)
                    for parity, data in enumerate((even, odd)):
                        moved[
                            pl.ds(base + k * size + parity * half, half),
                            plane * LANES : (plane + 1) * LANES,
                        ] = jnp.where(inside, data, 0.0).astype(jnp.bfloat16)
            target = jnp.where(lane_row < size, rows[0], rows[1])
            row_one[:, pl.ds(base + pair * LANES, LANES)] = jnp.where(
                offset == target, 1.0, 0.0
            ).astype(jnp.bfloat16)
        return carry

    lax.fori_loop(0, n_sky, place_owner, 0)
    run = 2 * span if n_sky % 2 == 0 else span

    def gathered(rows):
        def add(index, sum_so_far):
            depth = pl.ds(pl.multiple_of(index * run, run), run)
            return sum_so_far + wide_dot(row_one[rows, depth], moved[depth, :])

        first = wide_dot(row_one[rows, :run], moved[:run, :])
        return lax.fori_loop(1, n_sky * span // run, add, first)

    edges[...] = gathered(slice(0, 4 * margin))

    @pl.when(has_above)
    def _():
        light_copy(True).start()

    @pl.when(has_below)
    def _():
        light_copy(False).start()

    def residual_of(image, seen, sky):
        decay = jnp.exp(-jnp.abs(image))
        model = sky + (jnp.maximum(image, 0.0) + jnp.log(1.0 + decay))
        numerator = jnp.where(image >= 0, 1.0, decay)
        return (seen - model) * numerator / (model * (1.0 + decay))

    def keep(value, start):
        rounded = value.astype(jnp.bfloat16).astype(jnp.float32)
        for plane in range(planes):
            reach[pl.ds(plane * canvas_rows + start, margin), :] = rounded[
                :, plane * LANES : (plane + 1) * LANES
            ]

    middle[...] = gathered(slice(4 * margin, canvas_rows))
    for load in loads[4:]:
        load.wait()

    def core_chunk(index, carry):
        start = pl.multiple_of(index * margin, margin)
        inner = pl.multiple_of(start + margin, margin)
        value = residual_of(
            middle[pl.ds(start, margin), :],
            observed_here[pl.ds(inner, margin), :],
            background_here[pl.ds(inner, margin), :],
        )
        residual_out[0, pl.ds(inner, margin), :] = value
        keep(value, pl.multiple_of(start + 2 * margin, margin))
        return carry

    lax.fori_loop(0, canvas_rows // margin - 4, core_chunk, 0)
    reach[planes * canvas_rows :, :] = jnp.zeros((canvas_rows, LANES), jnp.float32)

    @pl.when(has_above)
    def _():
        light_copy(True).wait_send()
        light_copy(False).wait_recv()
        for copy in halo_copies(True):
            copy.wait_send()
        for copy in halo_copies(False):
            copy.wait_recv()

    @pl.when(has_below)
    def _():
        light_copy(False).wait_send()
        light_copy(True).wait_recv()
        for copy in halo_copies(False):
            copy.wait_send()
        for copy in halo_copies(True):
            copy.wait_recv()

    for slot, exists in ((0, has_above), (1, has_below)):
        outer = 0 if slot == 0 else canvas_rows - margin
        inner = margin if slot == 0 else canvas_rows - 2 * margin
        outer_light = 0 if slot == 0 else margin
        inner_light = margin - outer_light
        value = residual_of(
            edges[pl.ds(2 * slot * margin + outer_light, margin), :]
            + light_halo[slot, pl.ds(outer_light, margin), :],
            observed_halo[slot],
            background_halo[slot],
        )
        keep(jnp.where(exists, value, 0.0), outer)
        value = residual_of(
            edges[pl.ds(2 * slot * margin + inner_light, margin), :]
            + light_halo[slot, pl.ds(inner_light, margin), :],
            observed_here[pl.ds(inner - margin, margin), :],
            background_here[pl.ds(inner - margin, margin), :],
        )
        residual_out[0, pl.ds(inner - margin, margin), :] = value
        keep(value, inner)

    def pick_owner(owner, carry):
        def pick(k, inner_carry):
            col = stamp_col[0, owner, k]
            row = stamp_row[0, owner, k]
            shift = col & (LANES - 1)
            first = (col >> 7) * canvas_rows + row
            back = (LANES - shift) & (LANES - 1)
            halves = []
            for parity in range(2):
                near = reach[pl.ds(first + parity, half, stride=2), :]
                far = reach[pl.ds(first + canvas_rows + parity, half, stride=2), :]
                halves.append(jnp.where(lane_row >= shift, near, far))
            even = pltpu.roll(halves[0], back, 1)
            odd = pltpu.roll(pltpu.roll(halves[1], back, 1), size, 1)
            stamps[pl.ds(owner * capacity + k, half, stride=slot_pitch), :] = jnp.where(
                lane_half, even, odd
            )
            return inner_carry

        return lax.fori_loop(0, capacity, pick, carry, unroll=capacity)

    lax.fori_loop(0, n_sky, pick_owner, 0)
    for pair in range(pairs):
        windows[:, pair * LANES : (pair + 1) * LANES] = stamps[
            pl.ds(pair * slot_pitch, slots), :
        ].astype(jnp.bfloat16)
    both = wide_dot(windows[...], rendered[...], (((1,), (1,)), ((), ())))
    slot_grad[...] = jnp.where(live > 0, both[:, :n_par] + both[:, n_par:], 0.0)

    def reduce_copy(step):
        other = wrapped(me_e + step, n_epoch)
        return pltpu.make_async_remote_copy(
            src_ref=slot_grad.at[pl.ds(pl.multiple_of(other * per, per), per)],
            dst_ref=reduce_in.at[step],
            send_sem=reduce_send.at[step],
            recv_sem=reduce_recv.at[step],
            device_id=(me_s, other),
            device_id_type=MESH,
        )

    for step in range(1, n_epoch):
        reduce_copy(step).start()
    summed = slot_grad[pl.ds(pl.multiple_of(me_e * per, per), per), :]
    for step in range(1, n_epoch):
        reduce_copy(step).wait_recv()
        summed = summed + reduce_in[step]
    piece[...] = summed
    my_place = me_s * ratio + lax.rem(me_e, ratio)

    def gather_copy(step):
        return pltpu.make_async_remote_copy(
            src_ref=piece,
            dst_ref=gather_in.at[my_place],
            send_sem=gather_send.at[step],
            recv_sem=gather_recv.at[my_place],
            device_id=(my_owner, wrapped(me_e + step, n_epoch)),
            device_id_type=MESH,
        )

    for step in range(1, n_epoch):
        gather_copy(step).start()

    @pl.when(my_owner == me_s)
    def _():
        gather_in[my_place] = piece[...]

    @pl.when(my_owner != me_s)
    def _():
        gather_copy(0).start()

    for step in range(1, n_epoch):
        reduce_copy(step).wait_send()
        gather_copy(step).wait_send()

    @pl.when(my_owner != me_s)
    def _():
        gather_copy(0).wait_send()

    for tile in range(n_sky):
        for part in range(ratio):

            @pl.when(jnp.logical_not((me_s == tile) & (me_s * ratio + part == me_e)))
            def _():
                place = tile * ratio + part
                pltpu.make_async_remote_copy(
                    src_ref=piece,
                    dst_ref=gather_in.at[place],
                    send_sem=gather_send.at[0],
                    recv_sem=gather_recv.at[place],
                    device_id=(tile, me_s * ratio + part),
                    device_id_type=MESH,
                ).wait_recv()

    back = gather_in[...].reshape(slots, n_par)
    grad_out[...] = lax.dot_general(
        back,
        table,
        (((0,), (0,)), ((), ())),
        precision=lax.Precision.HIGHEST,
        preferred_element_type=jnp.float32,
    )


def on_device(
    n_sky,
    n_epoch,
    params,
    basis,
    psf_taps,
    send_index,
    tile_count,
    stamp_row,
    stamp_col,
    observed,
    background,
):
    n_par, pixels = basis.shape
    capacity = send_index.shape[2]
    slots = n_sky * capacity
    tile_rows, width = observed.shape[1:]
    size = 64
    margin = size // 2
    canvas_rows = tile_rows + 2 * margin
    planes = width // LANES
    pairs = pixels // LANES
    per = slots // n_epoch
    ratio = capacity // per
    f32, bf16 = jnp.float32, jnp.bfloat16
    vmem = pl.BlockSpec(memory_space=pltpu.VMEM)
    smem = pl.BlockSpec(memory_space=pltpu.SMEM)
    dma = pltpu.SemaphoreType.DMA
    hbm = pl.BlockSpec(memory_space=pltpu.HBM)
    param_grad, residual = pl.pallas_call(
        functools.partial(kernel, n_sky, n_epoch),
        out_shape=(
            jax.ShapeDtypeStruct((n_par, params.shape[0]), f32),
            jax.ShapeDtypeStruct(observed.shape, f32),
        ),
        in_specs=[vmem, hbm, smem, vmem, smem, smem, smem, smem, hbm, hbm],
        out_specs=(vmem, vmem),
        scratch_shapes=[
            pltpu.VMEM((n_sky, capacity, n_par), bf16),
            pltpu.VMEM((n_sky, capacity, n_par), bf16),
            pltpu.VMEM((2, margin, width), f32),
            pltpu.VMEM((2, margin, width), f32),
            pltpu.VMEM((n_par, pixels), bf16),
            pltpu.VMEM((tile_rows, width), f32),
            pltpu.VMEM((tile_rows, width), f32),
            pltpu.VMEM((pairs * (n_par + 8), LANES), f32),
            pltpu.VMEM((size, 8 * LANES), bf16),
            pltpu.VMEM((pairs * (n_par + 8), LANES), f32),
            pltpu.VMEM((2 * n_par, pixels), bf16),
            pltpu.VMEM((pairs * (slots + 8), LANES), f32),
            pltpu.VMEM((canvas_rows, slots * size), bf16),
            pltpu.VMEM((slots * size, width), bf16),
            pltpu.VMEM((4 * margin, width), f32),
            pltpu.VMEM((tile_rows - 2 * margin, width), f32),
            pltpu.VMEM((2, 2 * margin, width), f32),
            pltpu.VMEM(((planes + 1) * canvas_rows, LANES), f32),
            pltpu.VMEM((slots, pixels), bf16),
            pltpu.VMEM((slots, n_par), f32),
            pltpu.VMEM((n_epoch, per, n_par), f32),
            pltpu.VMEM((per, n_par), f32),
            pltpu.VMEM((n_sky * ratio, per, n_par), f32),
            dma((6,)),
            dma((n_sky,)),
            dma((n_sky,)),
            dma((2, 2)),
            dma((2, 2)),
            dma((2,)),
            dma((2,)),
            dma((n_epoch,)),
            dma((n_epoch,)),
            dma((n_epoch,)),
            dma((n_sky * ratio,)),
        ],
        compiler_params=pltpu.CompilerParams(
            collective_id=0, has_side_effects=True, vmem_limit_bytes=56 * 1024 * 1024
        ),
    )(
        params.T,
        basis,
        psf_taps,
        psf_taps,
        send_index,
        tile_count,
        stamp_row,
        stamp_col,
        observed,
        background,
    )
    return param_grad.T, residual


def solution(mesh):
    in_specs = (
        P("sky", None),
        P(),
        P("epoch", None, None),
        P("sky", None, None),
        P("sky", None),
        P("sky", None, None),
        P("sky", None, None),
        P("epoch", "sky", None),
        P("epoch", "sky", None),
    )
    out_specs = (P("sky", None), P("epoch", "sky", None))
    return jax.shard_map(
        functools.partial(on_device, mesh.shape["sky"], mesh.shape["epoch"]),
        mesh=mesh,
        in_specs=in_specs,
        out_specs=out_specs,
        check_vma=False,
    )
```

```python
import functools

import jax
import jax.numpy as jnp
from jax import lax
from jax.experimental import pallas as pl
from jax.experimental.pallas import tpu as pltpu
from jax.sharding import PartitionSpec as P

MESH = pl.DeviceIdType.MESH
LANES = 128


def split_two(value):
    high = value.astype(jnp.bfloat16)
    return high, (value - high.astype(jnp.float32)).astype(jnp.bfloat16)


def wrapped(value, count):
    return jnp.where(value >= count, value - count, value)


def wide_dot(left, right, dims=(((1,), (0,)), ((), ()))):
    return lax.dot_general(left, right, dims, preferred_element_type=jnp.float32)


def kernel(
    n_sky,
    n_epoch,
    params,
    basis,
    taps_scalar,
    taps_vector,
    send_index,
    tile_count,
    stamp_row,
    stamp_col,
    observed,
    background,
    grad_out,
    residual_out,
    outgoing,
    incoming,
    observed_halo,
    background_halo,
    basis_here,
    observed_here,
    background_here,
    basis_rows,
    basis_mixed,
    rendered_rows,
    rendered,
    stamps,
    row_one,
    moved,
    edges,
    middle,
    light_halo,
    reach,
    windows,
    slot_grad,
    reduce_in,
    piece,
    gather_in,
    load_sem,
    param_send,
    param_recv,
    halo_send,
    halo_recv,
    light_send,
    light_recv,
    reduce_send,
    reduce_recv,
    gather_send,
    gather_recv,
):
    me_s = lax.axis_index("sky")
    me_e = lax.axis_index("epoch")
    n_par, n_source = params.shape
    size = 64
    half = size // 2
    capacity = send_index.shape[2]
    slots = n_sky * capacity
    tile_rows = observed.shape[1]
    width = observed.shape[2]
    margin = half
    canvas_rows = tile_rows + 2 * margin
    planes = width // LANES
    pairs = size * size // LANES
    per = slots // n_epoch
    ratio = capacity // per
    n_taps = taps_vector.shape[2]
    reach_taps = (n_taps - 1) // 2
    my_owner = me_e // ratio
    slot_pitch = slots + 8
    par_pitch = n_par + 8
    has_above = me_s > 0
    has_below = me_s < n_sky - 1

    loads = [
        pltpu.make_async_copy(
            basis.at[pl.ds(part * (n_par // 4), n_par // 4)],
            basis_here.at[pl.ds(part * (n_par // 4), n_par // 4)],
            load_sem.at[part],
        )
        for part in range(4)
    ] + [
        pltpu.make_async_copy(observed.at[0], observed_here, load_sem.at[4]),
        pltpu.make_async_copy(background.at[0], background_here, load_sem.at[5]),
    ]
    for load in loads:
        load.start()

    barrier = pltpu.get_barrier_semaphore()
    for step in range(1, n_sky):
        pl.semaphore_signal(
            barrier, 1, device_id=(wrapped(me_s + step, n_sky), me_e), device_id_type=MESH
        )
    for step in range(1, n_epoch):
        pl.semaphore_signal(
            barrier, 1, device_id=(me_s, wrapped(me_e + step, n_epoch)), device_id_type=MESH
        )
    for tile in range(n_sky):
        for part in range(ratio):
            sender = me_s * ratio + part

            @pl.when(jnp.logical_not((me_s == tile) & (sender == me_e)))
            def _():
                pl.semaphore_signal(barrier, 1, device_id=(tile, sender), device_id_type=MESH)

    slot_at = lax.broadcasted_iota(jnp.int32, (8, n_source), 0)
    source_at = lax.broadcasted_iota(jnp.int32, (8, n_source), 1)
    rows_of = []
    for base in range(0, slots, 8):
        named = jnp.zeros_like(slot_at)
        for inner in range(8):
            tile, k = divmod(base + inner, capacity)
            named = jnp.where(slot_at == inner, send_index[0, tile, k], named)
        rows_of.append(jnp.where(named == source_at, 1.0, 0.0))
    table = jnp.concatenate(rows_of, axis=0)
    picked = wide_dot(
        table.astype(jnp.bfloat16), params[...], (((1,), (1,)), ((), ()))
    ).astype(jnp.bfloat16)
    for tile in range(n_sky):
        outgoing[tile] = picked[tile * capacity : (tile + 1) * capacity]
    incoming[me_s] = outgoing[me_s]

    def param_copy(step):
        other = wrapped(me_s + step, n_sky)
        return pltpu.make_async_remote_copy(
            src_ref=outgoing.at[other],
            dst_ref=incoming.at[me_s],
            send_sem=param_send.at[step],
            recv_sem=param_recv.at[step],
            device_id=(other, me_e),
            device_id_type=MESH,
        )

    def halo_copies(upward):
        other = me_s - 1 if upward else me_s + 1
        start = 0 if upward else tile_rows - margin
        slot = 1 if upward else 0
        return [
            pltpu.make_async_remote_copy(
                src_ref=array.at[0, pl.ds(start, margin)],
                dst_ref=landing.at[slot],
                send_sem=halo_send.at[which, slot],
                recv_sem=halo_recv.at[which, slot],
                device_id=(other, me_e),
                device_id_type=MESH,
            )
            for which, (array, landing) in enumerate(
                ((observed, observed_halo), (background, background_halo))
            )
        ]

    def light_copy(upward):
        other = me_s - 1 if upward else me_s + 1
        start = 0 if upward else 2 * margin
        slot = 1 if upward else 0
        return pltpu.make_async_remote_copy(
            src_ref=edges.at[pl.ds(start, 2 * margin)],
            dst_ref=light_halo.at[slot],
            send_sem=light_send.at[slot],
            recv_sem=light_recv.at[slot],
            device_id=(other, me_e),
            device_id_type=MESH,
        )

    @pl.when(jnp.logical_not(has_above))
    def _():
        light_halo[0] = jnp.zeros(light_halo.shape[1:], jnp.float32)
        observed_halo[0] = jnp.zeros(observed_halo.shape[1:], jnp.float32)
        background_halo[0] = jnp.ones(background_halo.shape[1:], jnp.float32)

    @pl.when(jnp.logical_not(has_below))
    def _():
        light_halo[1] = jnp.zeros(light_halo.shape[1:], jnp.float32)
        observed_halo[1] = jnp.zeros(observed_halo.shape[1:], jnp.float32)
        background_halo[1] = jnp.ones(background_halo.shape[1:], jnp.float32)

    def natural(value):
        return 2 * (value & (half - 1)) + (value >> 5)

    row_a = natural(lax.broadcasted_iota(jnp.int32, (size, size), 0))
    row_b = natural(lax.broadcasted_iota(jnp.int32, (size, size), 1))
    row_where = row_a - row_b + reach_taps
    col_c = lax.broadcasted_iota(jnp.int32, (size, size), 0)
    col_d = lax.broadcasted_iota(jnp.int32, (size, size), 1)
    col_where = col_d - col_c + reach_taps

    def tap_step(tap, both):
        row_k, col_k = both
        return (
            jnp.where(row_where == tap, taps_scalar[0, 0, tap], row_k),
            jnp.where(col_where == tap, taps_scalar[0, 1, tap], col_k),
        )

    row_k, col_k = lax.fori_loop(
        0,
        n_taps,
        tap_step,
        (jnp.zeros((size, size), jnp.float32), jnp.zeros((size, size), jnp.float32)),
        unroll=17 if n_taps % 17 == 0 else 1,
    )
    total = jnp.sum(taps_vector[0], axis=1, keepdims=True)
    row_high, row_low = split_two(row_k / total[0:1])
    col_k = col_k / total[1:2]
    blank = jnp.zeros_like(col_k)
    col_k = jnp.concatenate(
        [jnp.concatenate([col_k, blank], axis=1), jnp.concatenate([blank, col_k], axis=1)], axis=0
    )
    col_high, col_low = split_two(col_k)
    row_both = jnp.concatenate([row_high, row_low], axis=0)
    col_both = jnp.concatenate(
        [
            jnp.concatenate([col_high, col_low], axis=1),
            jnp.concatenate([col_high, jnp.zeros_like(col_low)], axis=1),
        ],
        axis=0,
    )

    pl.semaphore_wait(
        barrier,
        (n_sky - 1) + (n_epoch - 1) + n_epoch - jnp.where(my_owner == me_s, 1, 0),
    )

    for step in range(1, n_sky):
        param_copy(step).start()

    @pl.when(has_above)
    def _():
        for copy in halo_copies(True):
            copy.start()

    @pl.when(has_below)
    def _():
        for copy in halo_copies(False):
            copy.start()

    for load in loads[:4]:
        load.wait()
    lane_half = lax.broadcasted_iota(jnp.int32, (half, LANES), 1) < size
    for pair in range(pairs):
        basis_rows[pl.ds(pair * par_pitch, n_par), :] = basis_here[
            :, pair * LANES : (pair + 1) * LANES
        ].astype(jnp.float32)

    def swapped(one, two):
        return (
            jnp.where(lane_half, one, pltpu.roll(two, size, 1)),
            jnp.where(lane_half, pltpu.roll(one, size, 1), two),
        )

    group = 8

    for index in range(n_par // 2 // group):
        for inner in range(group):
            pp = index * group + inner
            one = basis_rows[pl.ds(2 * pp, half, stride=par_pitch), :]
            two = basis_rows[pl.ds(2 * pp + 1, half, stride=par_pitch), :]
            first, second = swapped(one, two)
            basis_mixed[:half, pp * LANES : (pp + 1) * LANES] = first.astype(jnp.bfloat16)
            basis_mixed[half:, pp * LANES : (pp + 1) * LANES] = second.astype(jnp.bfloat16)
    for index in range(n_par // 2 // group):
        by_row = wide_dot(
            row_both, basis_mixed[:, index * group * LANES : (index + 1) * group * LANES]
        )
        by_row = by_row[:size] + by_row[size:]
        tall = jnp.concatenate(
            [by_row[:, inner * LANES : (inner + 1) * LANES] for inner in range(group)], axis=0
        )
        high, low = split_two(tall)
        done = wide_dot(jnp.concatenate([high, low], axis=1), col_both)
        done = done[:, :LANES] + done[:, LANES:]
        for inner in range(group):
            pp = index * group + inner
            base = inner * size
            first, second = swapped(done[base : base + half], done[base + half : base + size])
            rendered_rows[pl.ds(2 * pp, half, stride=par_pitch), :] = first
            rendered_rows[pl.ds(2 * pp + 1, half, stride=par_pitch), :] = second
    for pair in range(pairs):
        high, low = split_two(rendered_rows[pl.ds(pair * par_pitch, n_par), :])
        rendered[:n_par, pair * LANES : (pair + 1) * LANES] = high
        rendered[n_par:, pair * LANES : (pair + 1) * LANES] = low

    for step in range(1, n_sky):
        copy = param_copy(step)
        copy.wait()
    par_slot = lax.broadcasted_iota(jnp.int32, (slots, n_par), 0)
    live = jnp.zeros((slots, n_par), jnp.float32)
    for owner in range(n_sky):
        inside = (par_slot >= owner * capacity) & (
            par_slot < owner * capacity + tile_count[0, owner]
        )
        live = jnp.where(inside & (par_slot < (owner + 1) * capacity), 1.0, live)
    here = incoming[...].reshape(slots, n_par).astype(jnp.float32)
    here = jnp.where(live > 0, here, 0.0)
    here = jnp.concatenate([here, here], axis=1).astype(jnp.bfloat16)
    wide = 8
    for block in range(pairs // wide):
        lanes = slice(block * wide * LANES, (block + 1) * wide * LANES)
        made = wide_dot(here, rendered[:, lanes])
        for inner in range(wide):
            stamps[pl.ds((block * wide + inner) * slot_pitch, slots), :] = made[
                :, inner * LANES : (inner + 1) * LANES
            ]

    lane_row = lax.broadcasted_iota(jnp.int32, (1, LANES), 1)
    level = lax.broadcasted_iota(jnp.int32, (canvas_rows, LANES), 0)
    level = jnp.where(
        level < 2 * margin,
        level,
        jnp.where(level < 4 * margin, level + (canvas_rows - 4 * margin), level - 2 * margin),
    )
    offset = level - natural(lane_row & (size - 1))
    span = capacity * size

    def place_owner(owner, carry):
        base = pl.multiple_of(owner * span, span)
        for pair in range(capacity // 2):
            rows = []
            for which in range(2):
                k = 2 * pair + which
                col = stamp_col[0, owner, k]
                rows.append(stamp_row[0, owner, k])
                stamp = stamps[pl.ds(owner * capacity + k, half, stride=slot_pitch), :]
                even = pltpu.roll(stamp, col & (LANES - 1), 1)
                odd = pltpu.roll(even, size, 1)
                for plane in range(planes):
                    at = lane_row + (plane * LANES) - col
                    inside = (at >= 0) & (at < size)
                    for parity, data in enumerate((even, odd)):
                        moved[
                            pl.ds(base + k * size + parity * half, half),
                            plane * LANES : (plane + 1) * LANES,
                        ] = jnp.where(inside, data, 0.0).astype(jnp.bfloat16)
            target = jnp.where(lane_row < size, rows[0], rows[1])
            row_one[:, pl.ds(base + pair * LANES, LANES)] = jnp.where(
                offset == target, 1.0, 0.0
            ).astype(jnp.bfloat16)
        return carry

    lax.fori_loop(0, n_sky, place_owner, 0)
    run = 2 * span if n_sky % 2 == 0 else span

    def gathered(rows):
        def add(index, sum_so_far):
            depth = pl.ds(pl.multiple_of(index * run, run), run)
            return sum_so_far + wide_dot(row_one[rows, depth], moved[depth, :])

        first = wide_dot(row_one[rows, :run], moved[:run, :])
        return lax.fori_loop(1, n_sky * span // run, add, first)

    edges[...] = gathered(slice(0, 4 * margin))

    @pl.when(has_above)
    def _():
        light_copy(True).start()

    @pl.when(has_below)
    def _():
        light_copy(False).start()

    def residual_of(image, seen, sky):
        decay = jnp.exp(-jnp.abs(image))
        model = sky + (jnp.maximum(image, 0.0) + jnp.log(1.0 + decay))
        numerator = jnp.where(image >= 0, 1.0, decay)
        return (seen - model) * numerator / (model * (1.0 + decay))

    def keep(value, start):
        rounded = value.astype(jnp.bfloat16).astype(jnp.float32)
        for plane in range(planes):
            reach[pl.ds(plane * canvas_rows + start, margin), :] = rounded[
                :, plane * LANES : (plane + 1) * LANES
            ]

    middle[...] = gathered(slice(4 * margin, canvas_rows))
    for load in loads[4:]:
        load.wait()

    def core_chunk(index, carry):
        start = pl.multiple_of(index * margin, margin)
        inner = pl.multiple_of(start + margin, margin)
        value = residual_of(
            middle[pl.ds(start, margin), :],
            observed_here[pl.ds(inner, margin), :],
            background_here[pl.ds(inner, margin), :],
        )
        residual_out[0, pl.ds(inner, margin), :] = value
        keep(value, pl.multiple_of(start + 2 * margin, margin))
        return carry

    lax.fori_loop(0, canvas_rows // margin - 4, core_chunk, 0, unroll=3)
    reach[planes * canvas_rows :, :] = jnp.zeros((canvas_rows, LANES), jnp.float32)

    @pl.when(has_above)
    def _():
        light_copy(True).wait_send()
        light_copy(False).wait_recv()
        for copy in halo_copies(True):
            copy.wait_send()
        for copy in halo_copies(False):
            copy.wait_recv()

    @pl.when(has_below)
    def _():
        light_copy(False).wait_send()
        light_copy(True).wait_recv()
        for copy in halo_copies(False):
            copy.wait_send()
        for copy in halo_copies(True):
            copy.wait_recv()

    for slot, exists in ((0, has_above), (1, has_below)):
        outer = 0 if slot == 0 else canvas_rows - margin
        inner = margin if slot == 0 else canvas_rows - 2 * margin
        outer_light = 0 if slot == 0 else margin
        inner_light = margin - outer_light
        value = residual_of(
            edges[pl.ds(2 * slot * margin + outer_light, margin), :]
            + light_halo[slot, pl.ds(outer_light, margin), :],
            observed_halo[slot],
            background_halo[slot],
        )
        keep(jnp.where(exists, value, 0.0), outer)
        value = residual_of(
            edges[pl.ds(2 * slot * margin + inner_light, margin), :]
            + light_halo[slot, pl.ds(inner_light, margin), :],
            observed_here[pl.ds(inner - margin, margin), :],
            background_here[pl.ds(inner - margin, margin), :],
        )
        residual_out[0, pl.ds(inner - margin, margin), :] = value
        keep(value, inner)

    def pick_owner(owner, carry):
        def pick(k, inner_carry):
            col = stamp_col[0, owner, k]
            row = stamp_row[0, owner, k]
            shift = col & (LANES - 1)
            first = (col >> 7) * canvas_rows + row
            back = (LANES - shift) & (LANES - 1)
            halves = []
            for parity in range(2):
                near = reach[pl.ds(first + parity, half, stride=2), :]
                far = reach[pl.ds(first + canvas_rows + parity, half, stride=2), :]
                halves.append(jnp.where(lane_row >= shift, near, far))
            even = pltpu.roll(halves[0], back, 1)
            odd = pltpu.roll(pltpu.roll(halves[1], back, 1), size, 1)
            stamps[pl.ds(owner * capacity + k, half, stride=slot_pitch), :] = jnp.where(
                lane_half, even, odd
            )
            return inner_carry

        return lax.fori_loop(0, capacity, pick, carry, unroll=capacity)

    lax.fori_loop(0, n_sky, pick_owner, 0)
    for pair in range(pairs):
        windows[:, pair * LANES : (pair + 1) * LANES] = stamps[
            pl.ds(pair * slot_pitch, slots), :
        ].astype(jnp.bfloat16)
    both = wide_dot(windows[...], rendered[...], (((1,), (1,)), ((), ())))
    slot_grad[...] = jnp.where(live > 0, both[:, :n_par] + both[:, n_par:], 0.0)

    def reduce_copy(step):
        other = wrapped(me_e + step, n_epoch)
        return pltpu.make_async_remote_copy(
            src_ref=slot_grad.at[pl.ds(pl.multiple_of(other * per, per), per)],
            dst_ref=reduce_in.at[step],
            send_sem=reduce_send.at[step],
            recv_sem=reduce_recv.at[step],
            device_id=(me_s, other),
            device_id_type=MESH,
        )

    for step in range(1, n_epoch):
        reduce_copy(step).start()
    summed = slot_grad[pl.ds(pl.multiple_of(me_e * per, per), per), :]
    for step in range(1, n_epoch):
        reduce_copy(step).wait_recv()
        summed = summed + reduce_in[step]
    piece[...] = summed
    my_place = me_s * ratio + lax.rem(me_e, ratio)

    def gather_copy(step):
        return pltpu.make_async_remote_copy(
            src_ref=piece,
            dst_ref=gather_in.at[my_place],
            send_sem=gather_send.at[step],
            recv_sem=gather_recv.at[my_place],
            device_id=(my_owner, wrapped(me_e + step, n_epoch)),
            device_id_type=MESH,
        )

    for step in range(1, n_epoch):
        gather_copy(step).start()

    @pl.when(my_owner == me_s)
    def _():
        gather_in[my_place] = piece[...]

    @pl.when(my_owner != me_s)
    def _():
        gather_copy(0).start()

    for step in range(1, n_epoch):
        reduce_copy(step).wait_send()
        gather_copy(step).wait_send()

    @pl.when(my_owner != me_s)
    def _():
        gather_copy(0).wait_send()

    for tile in range(n_sky):
        for part in range(ratio):

            @pl.when(jnp.logical_not((me_s == tile) & (me_s * ratio + part == me_e)))
            def _():
                place = tile * ratio + part
                pltpu.make_async_remote_copy(
                    src_ref=piece,
                    dst_ref=gather_in.at[place],
                    send_sem=gather_send.at[0],
                    recv_sem=gather_recv.at[place],
                    device_id=(tile, me_s * ratio + part),
                    device_id_type=MESH,
                ).wait_recv()

    back = gather_in[...].reshape(slots, n_par)
    high = back.astype(jnp.bfloat16)
    rest = back - high.astype(jnp.float32)
    middle_part, low = split_two(rest)
    exact = table.astype(jnp.bfloat16)
    grad_out[...] = wide_dot(
        jnp.concatenate([high, middle_part, low], axis=0),
        jnp.concatenate([exact, exact, exact], axis=0),
        (((0,), (0,)), ((), ())),
    )


def finish(grad, residual, grad_out, residual_out, sems):
    parts = 4
    rows = residual.shape[1] // parts
    copies = [
        pltpu.make_async_copy(
            residual.at[0, pl.ds(part * rows, rows)],
            residual_out.at[0, pl.ds(part * rows, rows)],
            sems.at[part],
        )
        for part in range(parts)
    ] + [pltpu.make_async_copy(grad, grad_out, sems.at[parts])]
    for copy in copies:
        copy.start()
    for copy in copies:
        copy.wait()


def on_device(
    n_sky,
    n_epoch,
    params,
    basis,
    psf_taps,
    send_index,
    tile_count,
    stamp_row,
    stamp_col,
    observed,
    background,
):
    n_par, pixels = basis.shape
    capacity = send_index.shape[2]
    slots = n_sky * capacity
    tile_rows, width = observed.shape[1:]
    size = 64
    margin = size // 2
    canvas_rows = tile_rows + 2 * margin
    planes = width // LANES
    pairs = pixels // LANES
    per = slots // n_epoch
    ratio = capacity // per
    f32, bf16 = jnp.float32, jnp.bfloat16
    vmem = pl.BlockSpec(memory_space=pltpu.VMEM)
    smem = pl.BlockSpec(memory_space=pltpu.SMEM)
    dma = pltpu.SemaphoreType.DMA
    hbm = pl.BlockSpec(memory_space=pltpu.HBM)
    params = params.T
    params, basis, psf_taps, send_index, tile_count, stamp_row, stamp_col = (
        pltpu.with_memory_space_constraint(array, pltpu.HBM)
        for array in (params, basis, psf_taps, send_index, tile_count, stamp_row, stamp_col)
    )
    observed, background = (
        pltpu.with_memory_space_constraint(array, pltpu.HBM) for array in (observed, background)
    )
    param_grad, residual = pl.pallas_call(
        functools.partial(kernel, n_sky, n_epoch),
        out_shape=(
            jax.ShapeDtypeStruct((n_par, params.shape[1]), f32),
            jax.ShapeDtypeStruct(observed.shape, f32),
        ),
        in_specs=[vmem, hbm, smem, vmem, smem, smem, smem, smem, hbm, hbm],
        out_specs=(vmem, vmem),
        scratch_shapes=[
            pltpu.VMEM((n_sky, capacity, n_par), bf16),
            pltpu.VMEM((n_sky, capacity, n_par), bf16),
            pltpu.VMEM((2, margin, width), f32),
            pltpu.VMEM((2, margin, width), f32),
            pltpu.VMEM((n_par, pixels), bf16),
            pltpu.VMEM((tile_rows, width), f32),
            pltpu.VMEM((tile_rows, width), f32),
            pltpu.VMEM((pairs * (n_par + 8), LANES), f32),
            pltpu.VMEM((size, pixels), bf16),
            pltpu.VMEM((pairs * (n_par + 8), LANES), f32),
            pltpu.VMEM((2 * n_par, pixels), bf16),
            pltpu.VMEM((pairs * (slots + 8), LANES), f32),
            pltpu.VMEM((canvas_rows, slots * size), bf16),
            pltpu.VMEM((slots * size, width), bf16),
            pltpu.VMEM((4 * margin, width), f32),
            pltpu.VMEM((tile_rows - 2 * margin, width), f32),
            pltpu.VMEM((2, 2 * margin, width), f32),
            pltpu.VMEM(((planes + 1) * canvas_rows, LANES), f32),
            pltpu.VMEM((slots, pixels), bf16),
            pltpu.VMEM((slots, n_par), f32),
            pltpu.VMEM((n_epoch, per, n_par), f32),
            pltpu.VMEM((per, n_par), f32),
            pltpu.VMEM((n_sky * ratio, per, n_par), f32),
            dma((6,)),
            dma((n_sky,)),
            dma((n_sky,)),
            dma((2, 2)),
            dma((2, 2)),
            dma((2,)),
            dma((2,)),
            dma((n_epoch,)),
            dma((n_epoch,)),
            dma((n_epoch,)),
            dma((n_sky * ratio,)),
        ],
        compiler_params=pltpu.CompilerParams(
            collective_id=0, has_side_effects=True, vmem_limit_bytes=(14 * 1024 + slots * 160) * 1024
        ),
    )(
        params,
        basis,
        psf_taps,
        psf_taps,
        send_index,
        tile_count,
        stamp_row,
        stamp_col,
        observed,
        background,
    )
    param_grad, residual = pl.pallas_call(
        finish,
        out_shape=(
            jax.ShapeDtypeStruct(param_grad.shape, f32),
            jax.ShapeDtypeStruct(residual.shape, f32),
        ),
        in_specs=[vmem, vmem],
        out_specs=(hbm, hbm),
        scratch_shapes=[dma((5,))],
    )(param_grad, residual)
    return param_grad.T, residual


def solution(mesh):
    in_specs = (
        P("sky", None),
        P(),
        P("epoch", None, None),
        P("sky", None, None),
        P("sky", None),
        P("sky", None, None),
        P("sky", None, None),
        P("epoch", "sky", None),
        P("epoch", "sky", None),
    )
    out_specs = (P("sky", None), P("epoch", "sky", None))
    return jax.shard_map(
        functools.partial(on_device, mesh.shape["sky"], mesh.shape["epoch"]),
        mesh=mesh,
        in_specs=in_specs,
        out_specs=out_specs,
        check_vma=False,
    )
```

```python
import functools

import jax
import jax.numpy as jnp
from jax import lax
from jax.experimental import pallas as pl
from jax.experimental.pallas import tpu as pltpu
from jax.sharding import PartitionSpec as P

MESH = pl.DeviceIdType.MESH
LANES = 128


def split_two(value):
    high = value.astype(jnp.bfloat16)
    return high, (value - high.astype(jnp.float32)).astype(jnp.bfloat16)


def wrapped(value, count):
    return jnp.where(value >= count, value - count, value)


def wide_dot(left, right, dims=(((1,), (0,)), ((), ()))):
    return lax.dot_general(left, right, dims, preferred_element_type=jnp.float32)


def kernel(
    n_sky,
    n_epoch,
    params,
    basis,
    taps_scalar,
    taps_vector,
    send_index,
    tile_count,
    stamp_row,
    stamp_col,
    observed,
    background,
    grad_out,
    residual_out,
    outgoing,
    incoming,
    basis_here,
    observed_here,
    background_here,
    basis_rows,
    basis_mixed,
    rendered_rows,
    rendered,
    stamps,
    row_one,
    moved,
    edges,
    core,
    light_halo,
    edge_out,
    edge_in,
    reach,
    windows,
    slot_grad,
    reduce_in,
    piece,
    gather_in,
    load_sem,
    param_send,
    param_recv,
    halo_send,
    halo_recv,
    light_send,
    light_recv,
    reduce_send,
    reduce_recv,
    gather_send,
    gather_recv,
):
    me_s = lax.axis_index("sky")
    me_e = lax.axis_index("epoch")
    n_par, n_source = params.shape
    size = 64
    half = size // 2
    capacity = send_index.shape[2]
    slots = n_sky * capacity
    tile_rows = observed.shape[1]
    width = observed.shape[2]
    margin = half
    canvas_rows = tile_rows + 2 * margin
    planes = width // LANES
    pairs = size * size // LANES
    per = slots // n_epoch
    ratio = capacity // per
    n_taps = taps_vector.shape[2]
    reach_taps = (n_taps - 1) // 2
    my_owner = me_e // ratio
    slot_pitch = slots + 8
    par_pitch = n_par + 8
    has_above = me_s > 0
    has_below = me_s < n_sky - 1

    loads = [
        pltpu.make_async_copy(
            basis.at[pl.ds(part * (n_par // 4), n_par // 4)],
            basis_here.at[pl.ds(part * (n_par // 4), n_par // 4)],
            load_sem.at[part],
        )
        for part in range(4)
    ] + [
        pltpu.make_async_copy(observed.at[0], observed_here, load_sem.at[4]),
        pltpu.make_async_copy(background.at[0], background_here, load_sem.at[5]),
    ]
    for load in loads:
        load.start()

    barrier = pltpu.get_barrier_semaphore()
    for step in range(1, n_sky):
        pl.semaphore_signal(
            barrier, 1, device_id=(wrapped(me_s + step, n_sky), me_e), device_id_type=MESH
        )
    for step in range(1, n_epoch):
        pl.semaphore_signal(
            barrier, 1, device_id=(me_s, wrapped(me_e + step, n_epoch)), device_id_type=MESH
        )
    for tile in range(n_sky):
        for part in range(ratio):
            sender = me_s * ratio + part

            @pl.when(jnp.logical_not((me_s == tile) & (sender == me_e)))
            def _():
                pl.semaphore_signal(barrier, 1, device_id=(tile, sender), device_id_type=MESH)

    slot_at = lax.broadcasted_iota(jnp.int32, (8, n_source), 0)
    source_at = lax.broadcasted_iota(jnp.int32, (8, n_source), 1)
    rows_of = []
    for base in range(0, slots, 8):
        named = jnp.zeros_like(slot_at)
        for inner in range(8):
            tile, k = divmod(base + inner, capacity)
            named = jnp.where(slot_at == inner, send_index[0, tile, k], named)
        rows_of.append(jnp.where(named == source_at, 1.0, 0.0))
    table = jnp.concatenate(rows_of, axis=0)
    picked = wide_dot(
        table.astype(jnp.bfloat16), params[...], (((1,), (1,)), ((), ()))
    ).astype(jnp.bfloat16)
    for tile in range(n_sky):
        outgoing[tile] = picked[tile * capacity : (tile + 1) * capacity]
    incoming[me_s] = outgoing[me_s]

    def param_copy(step):
        other = wrapped(me_s + step, n_sky)
        return pltpu.make_async_remote_copy(
            src_ref=outgoing.at[other],
            dst_ref=incoming.at[me_s],
            send_sem=param_send.at[step],
            recv_sem=param_recv.at[step],
            device_id=(other, me_e),
            device_id_type=MESH,
        )

    def halo_copy(upward):
        other = me_s - 1 if upward else me_s + 1
        slot = 1 if upward else 0
        return pltpu.make_async_remote_copy(
            src_ref=edge_out.at[1 - slot],
            dst_ref=edge_in.at[slot],
            send_sem=halo_send.at[slot],
            recv_sem=halo_recv.at[slot],
            device_id=(other, me_e),
            device_id_type=MESH,
        )

    def light_copy(upward):
        other = me_s - 1 if upward else me_s + 1
        start = 0 if upward else margin
        slot = 1 if upward else 0
        return pltpu.make_async_remote_copy(
            src_ref=edges.at[pl.ds(start, margin)],
            dst_ref=light_halo.at[slot],
            send_sem=light_send.at[slot],
            recv_sem=light_recv.at[slot],
            device_id=(other, me_e),
            device_id_type=MESH,
        )

    @pl.when(jnp.logical_not(has_above))
    def _():
        light_halo[0] = jnp.zeros(light_halo.shape[1:], jnp.float32)
        edge_in[0] = jnp.zeros(edge_in.shape[1:], jnp.bfloat16)

    @pl.when(jnp.logical_not(has_below))
    def _():
        light_halo[1] = jnp.zeros(light_halo.shape[1:], jnp.float32)
        edge_in[1] = jnp.zeros(edge_in.shape[1:], jnp.bfloat16)

    def natural(value):
        return 2 * (value & (half - 1)) + (value >> 5)

    row_a = natural(lax.broadcasted_iota(jnp.int32, (size, size), 0))
    row_b = natural(lax.broadcasted_iota(jnp.int32, (size, size), 1))
    row_where = row_a - row_b + reach_taps
    col_c = lax.broadcasted_iota(jnp.int32, (size, size), 0)
    col_d = lax.broadcasted_iota(jnp.int32, (size, size), 1)
    col_where = col_d - col_c + reach_taps

    def tap_step(tap, both):
        row_k, col_k = both
        return (
            jnp.where(row_where == tap, taps_scalar[0, 0, tap], row_k),
            jnp.where(col_where == tap, taps_scalar[0, 1, tap], col_k),
        )

    row_k, col_k = lax.fori_loop(
        0,
        n_taps,
        tap_step,
        (jnp.zeros((size, size), jnp.float32), jnp.zeros((size, size), jnp.float32)),
        unroll=17 if n_taps % 17 == 0 else 1,
    )
    total = jnp.sum(taps_vector[0], axis=1, keepdims=True)
    row_high, row_low = split_two(row_k / total[0:1])
    col_k = col_k / total[1:2]
    blank = jnp.zeros_like(col_k)
    col_k = jnp.concatenate(
        [jnp.concatenate([col_k, blank], axis=1), jnp.concatenate([blank, col_k], axis=1)], axis=0
    )
    col_high, col_low = split_two(col_k)
    row_both = jnp.concatenate([row_high, row_low], axis=0)
    col_both = jnp.concatenate(
        [
            jnp.concatenate([col_high, col_low], axis=1),
            jnp.concatenate([col_high, jnp.zeros_like(col_low)], axis=1),
        ],
        axis=0,
    )

    pl.semaphore_wait(
        barrier,
        (n_sky - 1) + (n_epoch - 1) + n_epoch - jnp.where(my_owner == me_s, 1, 0),
    )

    for step in range(1, n_sky):
        param_copy(step).start()

    for load in loads[:4]:
        load.wait()
    lane_half = lax.broadcasted_iota(jnp.int32, (half, LANES), 1) < size
    for pair in range(pairs):
        basis_rows[pl.ds(pair * par_pitch, n_par), :] = basis_here[
            :, pair * LANES : (pair + 1) * LANES
        ].astype(jnp.float32)

    def swapped(one, two):
        return (
            jnp.where(lane_half, one, pltpu.roll(two, size, 1)),
            jnp.where(lane_half, pltpu.roll(one, size, 1), two),
        )

    group = 8

    for index in range(n_par // 2 // group):
        for inner in range(group):
            pp = index * group + inner
            one = basis_rows[pl.ds(2 * pp, half, stride=par_pitch), :]
            two = basis_rows[pl.ds(2 * pp + 1, half, stride=par_pitch), :]
            first, second = swapped(one, two)
            basis_mixed[:half, pp * LANES : (pp + 1) * LANES] = first.astype(jnp.bfloat16)
            basis_mixed[half:, pp * LANES : (pp + 1) * LANES] = second.astype(jnp.bfloat16)
    for index in range(n_par // 2 // group):
        by_row = wide_dot(
            row_both, basis_mixed[:, index * group * LANES : (index + 1) * group * LANES]
        )
        by_row = by_row[:size] + by_row[size:]
        tall = jnp.concatenate(
            [by_row[:, inner * LANES : (inner + 1) * LANES] for inner in range(group)], axis=0
        )
        high, low = split_two(tall)
        done = wide_dot(jnp.concatenate([high, low], axis=1), col_both)
        done = done[:, :LANES] + done[:, LANES:]
        for inner in range(group):
            pp = index * group + inner
            base = inner * size
            first, second = swapped(done[base : base + half], done[base + half : base + size])
            rendered_rows[pl.ds(2 * pp, half, stride=par_pitch), :] = first
            rendered_rows[pl.ds(2 * pp + 1, half, stride=par_pitch), :] = second
    for pair in range(pairs):
        high, low = split_two(rendered_rows[pl.ds(pair * par_pitch, n_par), :])
        rendered[:n_par, pair * LANES : (pair + 1) * LANES] = high
        rendered[n_par:, pair * LANES : (pair + 1) * LANES] = low

    for step in range(1, n_sky):
        copy = param_copy(step)
        copy.wait()
    par_slot = lax.broadcasted_iota(jnp.int32, (slots, n_par), 0)
    live = jnp.zeros((slots, n_par), jnp.float32)
    for owner in range(n_sky):
        inside = (par_slot >= owner * capacity) & (
            par_slot < owner * capacity + tile_count[0, owner]
        )
        live = jnp.where(inside & (par_slot < (owner + 1) * capacity), 1.0, live)
    here = incoming[...].reshape(slots, n_par).astype(jnp.float32)
    here = jnp.where(live > 0, here, 0.0)
    here = jnp.concatenate([here, here], axis=1).astype(jnp.bfloat16)
    wide = 8
    for block in range(pairs // wide):
        lanes = slice(block * wide * LANES, (block + 1) * wide * LANES)
        made = wide_dot(here, rendered[:, lanes])
        for inner in range(wide):
            stamps[pl.ds((block * wide + inner) * slot_pitch, slots), :] = made[
                :, inner * LANES : (inner + 1) * LANES
            ]

    lane_row = lax.broadcasted_iota(jnp.int32, (1, LANES), 1)
    level = lax.broadcasted_iota(jnp.int32, (canvas_rows, LANES), 0)
    level = jnp.where(
        level < margin,
        level,
        jnp.where(level < 2 * margin, level + tile_rows, level - margin),
    )
    offset = level - natural(lane_row & (size - 1))
    span = capacity * size

    def place_owner(owner, carry):
        base = pl.multiple_of(owner * span, span)
        for pair in range(capacity // 2):
            rows = []
            for which in range(2):
                k = 2 * pair + which
                col = stamp_col[0, owner, k]
                rows.append(stamp_row[0, owner, k])
                stamp = stamps[pl.ds(owner * capacity + k, half, stride=slot_pitch), :]
                even = pltpu.roll(stamp, col & (LANES - 1), 1)
                odd = pltpu.roll(even, size, 1)
                for plane in range(planes):
                    at = lane_row + (plane * LANES) - col
                    inside = (at >= 0) & (at < size)
                    for parity, data in enumerate((even, odd)):
                        moved[
                            pl.ds(base + k * size + parity * half, half),
                            plane * LANES : (plane + 1) * LANES,
                        ] = jnp.where(inside, data, 0.0).astype(jnp.bfloat16)
            target = jnp.where(lane_row < size, rows[0], rows[1])
            row_one[:, pl.ds(base + pair * LANES, LANES)] = jnp.where(
                offset == target, 1.0, 0.0
            ).astype(jnp.bfloat16)
        return carry

    lax.fori_loop(0, n_sky, place_owner, 0)
    run = 2 * span if n_sky % 2 == 0 else span

    def gathered(rows):
        def add(index, sum_so_far):
            depth = pl.ds(pl.multiple_of(index * run, run), run)
            return sum_so_far + wide_dot(row_one[rows, depth], moved[depth, :])

        first = wide_dot(row_one[rows, :run], moved[:run, :])
        return lax.fori_loop(1, n_sky * span // run, add, first)

    edges[...] = gathered(slice(0, 2 * margin))

    @pl.when(has_above)
    def _():
        light_copy(True).start()

    @pl.when(has_below)
    def _():
        light_copy(False).start()

    def residual_of(image, seen, sky):
        decay = jnp.exp(-jnp.abs(image))
        model = sky + (jnp.maximum(image, 0.0) + jnp.log(1.0 + decay))
        numerator = jnp.where(image >= 0, 1.0, decay)
        return (seen - model) * numerator / (model * (1.0 + decay))

    def keep(rounded, start):
        wide = rounded.astype(jnp.float32)
        for plane in range(planes):
            reach[pl.ds(plane * canvas_rows + start, margin), :] = wide[
                :, plane * LANES : (plane + 1) * LANES
            ]

    core[...] = gathered(slice(2 * margin, canvas_rows))
    for load in loads[4:]:
        load.wait()

    def chunk_residual(start, light):
        rows = pl.ds(start, margin)
        image = core[rows, :] if light is None else core[rows, :] + light
        value = residual_of(image, observed_here[rows, :], background_here[rows, :])
        residual_out[0, rows, :] = value
        rounded = value.astype(jnp.bfloat16)
        keep(rounded, pl.multiple_of(start + margin, margin))
        return rounded

    def core_chunk(index, carry):
        chunk_residual(pl.multiple_of(index * margin, margin), None)
        return carry

    chunks = tile_rows // margin
    lax.fori_loop(1, chunks // 2, core_chunk, 0, unroll=3)
    reach[planes * canvas_rows :, :] = jnp.zeros((canvas_rows, LANES), jnp.float32)

    @pl.when(has_above)
    def _():
        light_copy(False).wait_recv()

    edge_out[0] = chunk_residual(0, light_halo[0])

    @pl.when(has_above)
    def _():
        halo_copy(True).start()

    @pl.when(has_below)
    def _():
        light_copy(True).wait_recv()

    edge_out[1] = chunk_residual(tile_rows - margin, light_halo[1])

    @pl.when(has_below)
    def _():
        halo_copy(False).start()

    lax.fori_loop(chunks // 2, chunks - 1, core_chunk, 0, unroll=3)

    @pl.when(has_above)
    def _():
        light_copy(True).wait_send()
        halo_copy(True).wait_send()
        halo_copy(False).wait_recv()

    @pl.when(has_below)
    def _():
        light_copy(False).wait_send()
        halo_copy(False).wait_send()
        halo_copy(True).wait_recv()

    keep(edge_in[0], 0)
    keep(edge_in[1], canvas_rows - margin)

    def pick_owner(owner, carry):
        def pick(k, inner_carry):
            col = stamp_col[0, owner, k]
            row = stamp_row[0, owner, k]
            shift = col & (LANES - 1)
            first = (col >> 7) * canvas_rows + row
            back = (LANES - shift) & (LANES - 1)
            halves = []
            for parity in range(2):
                near = reach[pl.ds(first + parity, half, stride=2), :]
                far = reach[pl.ds(first + canvas_rows + parity, half, stride=2), :]
                halves.append(jnp.where(lane_row >= shift, near, far))
            even = pltpu.roll(halves[0], back, 1)
            odd = pltpu.roll(pltpu.roll(halves[1], back, 1), size, 1)
            stamps[pl.ds(owner * capacity + k, half, stride=slot_pitch), :] = jnp.where(
                lane_half, even, odd
            )
            return inner_carry

        return lax.fori_loop(0, capacity, pick, carry, unroll=capacity)

    lax.fori_loop(0, n_sky, pick_owner, 0)
    for pair in range(pairs):
        windows[:, pair * LANES : (pair + 1) * LANES] = stamps[
            pl.ds(pair * slot_pitch, slots), :
        ].astype(jnp.bfloat16)
    both = wide_dot(windows[...], rendered[...], (((1,), (1,)), ((), ())))
    slot_grad[...] = jnp.where(live > 0, both[:, :n_par] + both[:, n_par:], 0.0)

    def reduce_copy(step):
        other = wrapped(me_e + step, n_epoch)
        return pltpu.make_async_remote_copy(
            src_ref=slot_grad.at[pl.ds(pl.multiple_of(other * per, per), per)],
            dst_ref=reduce_in.at[step],
            send_sem=reduce_send.at[step],
            recv_sem=reduce_recv.at[step],
            device_id=(me_s, other),
            device_id_type=MESH,
        )

    for step in range(1, n_epoch):
        reduce_copy(step).start()
    summed = slot_grad[pl.ds(pl.multiple_of(me_e * per, per), per), :]
    for step in range(1, n_epoch):
        reduce_copy(step).wait_recv()
        summed = summed + reduce_in[step]
    piece[...] = summed
    my_place = me_s * ratio + lax.rem(me_e, ratio)

    def gather_copy(step):
        return pltpu.make_async_remote_copy(
            src_ref=piece,
            dst_ref=gather_in.at[my_place],
            send_sem=gather_send.at[step],
            recv_sem=gather_recv.at[my_place],
            device_id=(my_owner, wrapped(me_e + step, n_epoch)),
            device_id_type=MESH,
        )

    for step in range(1, n_epoch):
        gather_copy(step).start()

    @pl.when(my_owner == me_s)
    def _():
        gather_in[my_place] = piece[...]

    @pl.when(my_owner != me_s)
    def _():
        gather_copy(0).start()

    for step in range(1, n_epoch):
        reduce_copy(step).wait_send()
        gather_copy(step).wait_send()

    @pl.when(my_owner != me_s)
    def _():
        gather_copy(0).wait_send()

    for tile in range(n_sky):
        for part in range(ratio):

            @pl.when(jnp.logical_not((me_s == tile) & (me_s * ratio + part == me_e)))
            def _():
                place = tile * ratio + part
                pltpu.make_async_remote_copy(
                    src_ref=piece,
                    dst_ref=gather_in.at[place],
                    send_sem=gather_send.at[0],
                    recv_sem=gather_recv.at[place],
                    device_id=(tile, me_s * ratio + part),
                    device_id_type=MESH,
                ).wait_recv()

    back = gather_in[...].reshape(slots, n_par)
    high = back.astype(jnp.bfloat16)
    rest = back - high.astype(jnp.float32)
    middle_part, low = split_two(rest)
    exact = table.astype(jnp.bfloat16)
    grad_out[...] = wide_dot(
        jnp.concatenate([high, middle_part, low], axis=0),
        jnp.concatenate([exact, exact, exact], axis=0),
        (((0,), (0,)), ((), ())),
    )


def finish(grad, residual, grad_out, residual_out, sems):
    parts = 4
    rows = residual.shape[1] // parts
    copies = [
        pltpu.make_async_copy(
            residual.at[0, pl.ds(part * rows, rows)],
            residual_out.at[0, pl.ds(part * rows, rows)],
            sems.at[part],
        )
        for part in range(parts)
    ] + [pltpu.make_async_copy(grad, grad_out, sems.at[parts])]
    for copy in copies:
        copy.start()
    for copy in copies:
        copy.wait()


def on_device(
    n_sky,
    n_epoch,
    params,
    basis,
    psf_taps,
    send_index,
    tile_count,
    stamp_row,
    stamp_col,
    observed,
    background,
):
    n_par, pixels = basis.shape
    capacity = send_index.shape[2]
    slots = n_sky * capacity
    tile_rows, width = observed.shape[1:]
    size = 64
    margin = size // 2
    canvas_rows = tile_rows + 2 * margin
    planes = width // LANES
    pairs = pixels // LANES
    per = slots // n_epoch
    ratio = capacity // per
    f32, bf16 = jnp.float32, jnp.bfloat16
    vmem = pl.BlockSpec(memory_space=pltpu.VMEM)
    smem = pl.BlockSpec(memory_space=pltpu.SMEM)
    dma = pltpu.SemaphoreType.DMA
    hbm = pl.BlockSpec(memory_space=pltpu.HBM)
    params = params.T
    params, basis, psf_taps, send_index, tile_count, stamp_row, stamp_col = (
        pltpu.with_memory_space_constraint(array, pltpu.HBM)
        for array in (params, basis, psf_taps, send_index, tile_count, stamp_row, stamp_col)
    )
    observed, background = (
        pltpu.with_memory_space_constraint(array, pltpu.HBM) for array in (observed, background)
    )
    param_grad, residual = pl.pallas_call(
        functools.partial(kernel, n_sky, n_epoch),
        out_shape=(
            jax.ShapeDtypeStruct((n_par, params.shape[1]), f32),
            jax.ShapeDtypeStruct(observed.shape, f32),
        ),
        in_specs=[vmem, hbm, smem, vmem, smem, smem, smem, smem, hbm, hbm],
        out_specs=(vmem, vmem),
        scratch_shapes=[
            pltpu.VMEM((n_sky, capacity, n_par), bf16),
            pltpu.VMEM((n_sky, capacity, n_par), bf16),
            pltpu.VMEM((n_par, pixels), bf16),
            pltpu.VMEM((tile_rows, width), f32),
            pltpu.VMEM((tile_rows, width), f32),
            pltpu.VMEM((pairs * (n_par + 8), LANES), f32),
            pltpu.VMEM((size, pixels), bf16),
            pltpu.VMEM((pairs * (n_par + 8), LANES), f32),
            pltpu.VMEM((2 * n_par, pixels), bf16),
            pltpu.VMEM((pairs * (slots + 8), LANES), f32),
            pltpu.VMEM((canvas_rows, slots * size), bf16),
            pltpu.VMEM((slots * size, width), bf16),
            pltpu.VMEM((2 * margin, width), f32),
            pltpu.VMEM((tile_rows, width), f32),
            pltpu.VMEM((2, margin, width), f32),
            pltpu.VMEM((2, margin, width), bf16),
            pltpu.VMEM((2, margin, width), bf16),
            pltpu.VMEM(((planes + 1) * canvas_rows, LANES), f32),
            pltpu.VMEM((slots, pixels), bf16),
            pltpu.VMEM((slots, n_par), f32),
            pltpu.VMEM((n_epoch, per, n_par), f32),
            pltpu.VMEM((per, n_par), f32),
            pltpu.VMEM((n_sky * ratio, per, n_par), f32),
            dma((6,)),
            dma((n_sky,)),
            dma((n_sky,)),
            dma((2,)),
            dma((2,)),
            dma((2,)),
            dma((2,)),
            dma((n_epoch,)),
            dma((n_epoch,)),
            dma((n_epoch,)),
            dma((n_sky * ratio,)),
        ],
        compiler_params=pltpu.CompilerParams(
            collective_id=0, has_side_effects=True, vmem_limit_bytes=(14 * 1024 + slots * 160) * 1024
        ),
    )(
        params,
        basis,
        psf_taps,
        psf_taps,
        send_index,
        tile_count,
        stamp_row,
        stamp_col,
        observed,
        background,
    )
    param_grad, residual = pl.pallas_call(
        finish,
        out_shape=(
            jax.ShapeDtypeStruct(param_grad.shape, f32),
            jax.ShapeDtypeStruct(residual.shape, f32),
        ),
        in_specs=[vmem, vmem],
        out_specs=(hbm, hbm),
        scratch_shapes=[dma((5,))],
        compiler_params=pltpu.CompilerParams(vmem_limit_bytes=2 * 1024 * 1024),
    )(param_grad, residual)
    return param_grad.T, residual


def solution(mesh):
    in_specs = (
        P("sky", None),
        P(),
        P("epoch", None, None),
        P("sky", None, None),
        P("sky", None),
        P("sky", None, None),
        P("sky", None, None),
        P("epoch", "sky", None),
        P("epoch", "sky", None),
    )
    out_specs = (P("sky", None), P("epoch", "sky", None))
    return jax.shard_map(
        functools.partial(on_device, mesh.shape["sky"], mesh.shape["epoch"]),
        mesh=mesh,
        in_specs=in_specs,
        out_specs=out_specs,
        check_vma=False,
    )
```

```python
import functools

import jax
import jax.numpy as jnp
from jax import lax
from jax.experimental import pallas as pl
from jax.experimental.pallas import tpu as pltpu
from jax.sharding import PartitionSpec as P

MESH = pl.DeviceIdType.MESH
LANES = 128


def split_two(value):
    high = value.astype(jnp.bfloat16)
    return high, (value - high.astype(jnp.float32)).astype(jnp.bfloat16)


def wrapped(value, count):
    return jnp.where(value >= count, value - count, value)


def wide_dot(left, right, dims=(((1,), (0,)), ((), ()))):
    return lax.dot_general(left, right, dims, preferred_element_type=jnp.float32)


def kernel(
    n_sky,
    n_epoch,
    params,
    basis,
    taps_scalar,
    taps_vector,
    send_index,
    tile_count,
    stamp_row,
    stamp_col,
    observed,
    background,
    grad_out,
    residual_out,
    outgoing,
    incoming,
    observed_halo,
    background_halo,
    basis_here,
    observed_here,
    background_here,
    basis_rows,
    basis_mixed,
    rendered_rows,
    rendered,
    stamps,
    row_one,
    moved,
    edges,
    middle,
    light_halo,
    reach,
    windows,
    slot_grad,
    part_in,
    piece,
    gather_in,
    load_sem,
    param_send,
    param_recv,
    halo_send,
    halo_recv,
    light_send,
    light_recv,
    part_send,
    part_recv,
    gather_send,
    gather_recv,
):
    me_s = lax.axis_index("sky")
    me_e = lax.axis_index("epoch")
    n_par, n_source = params.shape
    size = 64
    half = size // 2
    capacity = send_index.shape[2]
    slots = n_sky * capacity
    tile_rows = observed.shape[1]
    width = observed.shape[2]
    margin = half
    canvas_rows = tile_rows + 2 * margin
    planes = width // LANES
    pairs = size * size // LANES
    per = capacity // 2
    n_taps = taps_vector.shape[2]
    reach_taps = (n_taps - 1) // 2
    me_core = lax.rem(me_e, 2)
    sibling = me_e + 1 - 2 * me_core
    slot_pitch = slots + 8
    par_pitch = n_par + 8
    has_above = me_s > 0
    has_below = me_s < n_sky - 1

    loads = [
        pltpu.make_async_copy(
            basis.at[pl.ds(part * (n_par // 4), n_par // 4)],
            basis_here.at[pl.ds(part * (n_par // 4), n_par // 4)],
            load_sem.at[part],
        )
        for part in range(4)
    ] + [
        pltpu.make_async_copy(observed.at[0], observed_here, load_sem.at[4]),
        pltpu.make_async_copy(background.at[0], background_here, load_sem.at[5]),
    ]
    for load in loads:
        load.start()

    barrier = pltpu.get_barrier_semaphore()
    for step in range(n_sky):
        for other in (me_e, sibling)[int(step == 0) :]:
            pl.semaphore_signal(
                barrier, 1, device_id=(wrapped(me_s + step, n_sky), other), device_id_type=MESH
            )
    for step in range(2, n_epoch):
        pl.semaphore_signal(
            barrier,
            1,
            device_id=(me_s, wrapped(me_e - me_core + step, n_epoch)),
            device_id_type=MESH,
        )

    slot_at = lax.broadcasted_iota(jnp.int32, (8, n_source), 0)
    source_at = lax.broadcasted_iota(jnp.int32, (8, n_source), 1)
    rows_of = []
    for base in range(0, slots, 8):
        named = jnp.zeros_like(slot_at)
        for inner in range(8):
            tile, k = divmod(base + inner, capacity)
            named = jnp.where(slot_at == inner, send_index[0, tile, k], named)
        rows_of.append(jnp.where(named == source_at, 1.0, 0.0))
    table = jnp.concatenate(rows_of, axis=0)
    picked = wide_dot(
        table.astype(jnp.bfloat16), params[...], (((1,), (1,)), ((), ()))
    ).astype(jnp.bfloat16)
    for tile in range(n_sky):
        outgoing[tile] = picked[tile * capacity : (tile + 1) * capacity]
    incoming[me_s] = outgoing[me_s]

    def param_copy(step):
        other = wrapped(me_s + step, n_sky)
        return pltpu.make_async_remote_copy(
            src_ref=outgoing.at[other],
            dst_ref=incoming.at[me_s],
            send_sem=param_send.at[step],
            recv_sem=param_recv.at[step],
            device_id=(other, me_e),
            device_id_type=MESH,
        )

    def halo_copies(upward):
        other = me_s - 1 if upward else me_s + 1
        start = 0 if upward else tile_rows - margin
        slot = 1 if upward else 0
        return [
            pltpu.make_async_remote_copy(
                src_ref=array.at[0, pl.ds(start, margin)],
                dst_ref=landing.at[slot],
                send_sem=halo_send.at[which, slot],
                recv_sem=halo_recv.at[which, slot],
                device_id=(other, me_e),
                device_id_type=MESH,
            )
            for which, (array, landing) in enumerate(
                ((observed, observed_halo), (background, background_halo))
            )
        ]

    def light_copy(upward):
        other = me_s - 1 if upward else me_s + 1
        start = 0 if upward else 2 * margin
        slot = 1 if upward else 0
        return pltpu.make_async_remote_copy(
            src_ref=edges.at[pl.ds(start, 2 * margin)],
            dst_ref=light_halo.at[slot],
            send_sem=light_send.at[slot],
            recv_sem=light_recv.at[slot],
            device_id=(other, me_e),
            device_id_type=MESH,
        )

    @pl.when(jnp.logical_not(has_above))
    def _():
        light_halo[0] = jnp.zeros(light_halo.shape[1:], jnp.float32)
        observed_halo[0] = jnp.zeros(observed_halo.shape[1:], jnp.float32)
        background_halo[0] = jnp.ones(background_halo.shape[1:], jnp.float32)

    @pl.when(jnp.logical_not(has_below))
    def _():
        light_halo[1] = jnp.zeros(light_halo.shape[1:], jnp.float32)
        observed_halo[1] = jnp.zeros(observed_halo.shape[1:], jnp.float32)
        background_halo[1] = jnp.ones(background_halo.shape[1:], jnp.float32)

    def natural(value):
        return 2 * (value & (half - 1)) + (value >> 5)

    row_a = natural(lax.broadcasted_iota(jnp.int32, (size, size), 0))
    row_b = natural(lax.broadcasted_iota(jnp.int32, (size, size), 1))
    row_where = row_a - row_b + reach_taps
    col_c = lax.broadcasted_iota(jnp.int32, (size, size), 0)
    col_d = lax.broadcasted_iota(jnp.int32, (size, size), 1)
    col_where = col_d - col_c + reach_taps

    def tap_step(tap, both):
        row_k, col_k = both
        return (
            jnp.where(row_where == tap, taps_scalar[0, 0, tap], row_k),
            jnp.where(col_where == tap, taps_scalar[0, 1, tap], col_k),
        )

    row_k, col_k = lax.fori_loop(
        0,
        n_taps,
        tap_step,
        (jnp.zeros((size, size), jnp.float32), jnp.zeros((size, size), jnp.float32)),
        unroll=17 if n_taps % 17 == 0 else 1,
    )
    total = jnp.sum(taps_vector[0], axis=1, keepdims=True)
    row_high, row_low = split_two(row_k / total[0:1])
    col_k = col_k / total[1:2]
    blank = jnp.zeros_like(col_k)
    col_k = jnp.concatenate(
        [jnp.concatenate([col_k, blank], axis=1), jnp.concatenate([blank, col_k], axis=1)], axis=0
    )
    col_high, col_low = split_two(col_k)
    row_both = jnp.concatenate([row_high, row_low], axis=0)
    col_both = jnp.concatenate(
        [
            jnp.concatenate([col_high, col_low], axis=1),
            jnp.concatenate([col_high, jnp.zeros_like(col_low)], axis=1),
        ],
        axis=0,
    )

    pl.semaphore_wait(barrier, (2 * n_sky - 1) + (n_epoch - 2))
    for step in range(1, n_sky):
        param_copy(step).start()

    @pl.when(has_above)
    def _():
        for copy in halo_copies(True):
            copy.start()

    @pl.when(has_below)
    def _():
        for copy in halo_copies(False):
            copy.start()

    for load in loads[:4]:
        load.wait()
    lane_half = lax.broadcasted_iota(jnp.int32, (half, LANES), 1) < size
    for pair in range(pairs):
        basis_rows[pl.ds(pair * par_pitch, n_par), :] = basis_here[
            :, pair * LANES : (pair + 1) * LANES
        ].astype(jnp.float32)

    def swapped(one, two):
        return (
            jnp.where(lane_half, one, pltpu.roll(two, size, 1)),
            jnp.where(lane_half, pltpu.roll(one, size, 1), two),
        )

    group = 8

    for index in range(n_par // 2 // group):
        for inner in range(group):
            pp = index * group + inner
            one = basis_rows[pl.ds(2 * pp, half, stride=par_pitch), :]
            two = basis_rows[pl.ds(2 * pp + 1, half, stride=par_pitch), :]
            first, second = swapped(one, two)
            basis_mixed[:half, pp * LANES : (pp + 1) * LANES] = first.astype(jnp.bfloat16)
            basis_mixed[half:, pp * LANES : (pp + 1) * LANES] = second.astype(jnp.bfloat16)
    for index in range(n_par // 2 // group):
        by_row = wide_dot(
            row_both, basis_mixed[:, index * group * LANES : (index + 1) * group * LANES]
        )
        by_row = by_row[:size] + by_row[size:]
        tall = jnp.concatenate(
            [by_row[:, inner * LANES : (inner + 1) * LANES] for inner in range(group)], axis=0
        )
        high, low = split_two(tall)
        done = wide_dot(jnp.concatenate([high, low], axis=1), col_both)
        done = done[:, :LANES] + done[:, LANES:]
        for inner in range(group):
            pp = index * group + inner
            base = inner * size
            first, second = swapped(done[base : base + half], done[base + half : base + size])
            rendered_rows[pl.ds(2 * pp, half, stride=par_pitch), :] = first
            rendered_rows[pl.ds(2 * pp + 1, half, stride=par_pitch), :] = second
    for pair in range(pairs):
        high, low = split_two(rendered_rows[pl.ds(pair * par_pitch, n_par), :])
        rendered[:n_par, pair * LANES : (pair + 1) * LANES] = high
        rendered[n_par:, pair * LANES : (pair + 1) * LANES] = low

    for step in range(1, n_sky):
        copy = param_copy(step)
        copy.wait()
    par_slot = lax.broadcasted_iota(jnp.int32, (slots, n_par), 0)
    live = jnp.zeros((slots, n_par), jnp.float32)
    for owner in range(n_sky):
        inside = (par_slot >= owner * capacity) & (
            par_slot < owner * capacity + tile_count[0, owner]
        )
        live = jnp.where(inside & (par_slot < (owner + 1) * capacity), 1.0, live)
    here = incoming[...].reshape(slots, n_par).astype(jnp.float32)
    here = jnp.where(live > 0, here, 0.0)
    here = jnp.concatenate([here, here], axis=1).astype(jnp.bfloat16)
    wide = 8
    for block in range(pairs // wide):
        lanes = slice(block * wide * LANES, (block + 1) * wide * LANES)
        made = wide_dot(here, rendered[:, lanes])
        for inner in range(wide):
            stamps[pl.ds((block * wide + inner) * slot_pitch, slots), :] = made[
                :, inner * LANES : (inner + 1) * LANES
            ]

    lane_row = lax.broadcasted_iota(jnp.int32, (1, LANES), 1)
    level = lax.broadcasted_iota(jnp.int32, (canvas_rows, LANES), 0)
    level = jnp.where(
        level < 2 * margin,
        level,
        jnp.where(level < 4 * margin, level + (canvas_rows - 4 * margin), level - 2 * margin),
    )
    offset = level - natural(lane_row & (size - 1))
    offset = jnp.where(offset < 0, -1, jnp.where(offset > tile_rows, 2 * tile_rows, offset))
    offset = offset.astype(jnp.float32).astype(jnp.bfloat16)
    span = capacity * size

    def place_owner(owner, carry):
        base = pl.multiple_of(owner * span, span)
        for pair in range(capacity // 2):
            rows = []
            for which in range(2):
                k = 2 * pair + which
                col = stamp_col[0, owner, k]
                rows.append(stamp_row[0, owner, k])
                stamp = stamps[pl.ds(owner * capacity + k, half, stride=slot_pitch), :]
                even = pltpu.roll(stamp, col & (LANES - 1), 1)
                odd = pltpu.roll(even, size, 1).astype(jnp.bfloat16)
                even = even.astype(jnp.bfloat16)
                for plane in range(planes):
                    at = lane_row + (plane * LANES) - col
                    inside = jnp.where((at >= 0) & (at < size), 1.0, 0.0).astype(jnp.bfloat16)
                    for parity, data in enumerate((even, odd)):
                        moved[
                            pl.ds(base + k * size + parity * half, half),
                            plane * LANES : (plane + 1) * LANES,
                        ] = data * inside
            target = jnp.where(lane_row < size, rows[0], rows[1])
            target = target.astype(jnp.float32).astype(jnp.bfloat16)
            row_one[:, pl.ds(base + pair * LANES, LANES)] = jnp.where(
                offset == target, jnp.ones_like(offset), jnp.zeros_like(offset)
            )
        return carry

    lax.fori_loop(0, n_sky, place_owner, 0)
    run = 2 * span if n_sky % 2 == 0 else span

    def gathered(rows):
        def add(index, sum_so_far):
            depth = pl.ds(pl.multiple_of(index * run, run), run)
            return sum_so_far + wide_dot(row_one[rows, depth], moved[depth, :])

        first = wide_dot(row_one[rows, :run], moved[:run, :])
        return lax.fori_loop(1, n_sky * span // run, add, first)

    edges[...] = gathered(slice(0, 4 * margin))

    @pl.when(has_above)
    def _():
        light_copy(True).start()

    @pl.when(has_below)
    def _():
        light_copy(False).start()

    def residual_of(image, seen, sky):
        decay = jnp.exp(-jnp.abs(image))
        model = sky + (jnp.maximum(image, 0.0) + jnp.log(1.0 + decay))
        numerator = jnp.where(image >= 0, 1.0, decay)
        return (seen - model) * numerator / (model * (1.0 + decay))

    def keep(value, start):
        rounded = value.astype(jnp.bfloat16).astype(jnp.float32)
        for plane in range(planes):
            reach[pl.ds(plane * canvas_rows + start, margin), :] = rounded[
                :, plane * LANES : (plane + 1) * LANES
            ]

    middle[...] = gathered(slice(4 * margin, canvas_rows))
    for load in loads[4:]:
        load.wait()

    def core_chunk(index, carry):
        start = pl.multiple_of(index * margin, margin)
        inner = pl.multiple_of(start + margin, margin)
        value = residual_of(
            middle[pl.ds(start, margin), :],
            observed_here[pl.ds(inner, margin), :],
            background_here[pl.ds(inner, margin), :],
        )
        residual_out[0, pl.ds(inner, margin), :] = value
        keep(value, pl.multiple_of(start + 2 * margin, margin))
        return carry

    lax.fori_loop(0, canvas_rows // margin - 4, core_chunk, 0, unroll=3)
    reach[planes * canvas_rows :, :] = jnp.zeros((canvas_rows, LANES), jnp.float32)

    @pl.when(has_above)
    def _():
        light_copy(True).wait_send()
        light_copy(False).wait_recv()
        for copy in halo_copies(True):
            copy.wait_send()
        for copy in halo_copies(False):
            copy.wait_recv()

    @pl.when(has_below)
    def _():
        light_copy(False).wait_send()
        light_copy(True).wait_recv()
        for copy in halo_copies(False):
            copy.wait_send()
        for copy in halo_copies(True):
            copy.wait_recv()

    for slot, exists in ((0, has_above), (1, has_below)):
        outer = 0 if slot == 0 else canvas_rows - margin
        inner = margin if slot == 0 else canvas_rows - 2 * margin
        outer_light = 0 if slot == 0 else margin
        inner_light = margin - outer_light
        value = residual_of(
            edges[pl.ds(2 * slot * margin + outer_light, margin), :]
            + light_halo[slot, pl.ds(outer_light, margin), :],
            observed_halo[slot],
            background_halo[slot],
        )
        keep(jnp.where(exists, value, 0.0), outer)
        value = residual_of(
            edges[pl.ds(2 * slot * margin + inner_light, margin), :]
            + light_halo[slot, pl.ds(inner_light, margin), :],
            observed_here[pl.ds(inner - margin, margin), :],
            background_here[pl.ds(inner - margin, margin), :],
        )
        residual_out[0, pl.ds(inner - margin, margin), :] = value
        keep(value, inner)

    def pick_owner(owner, carry):
        def pick(k, inner_carry):
            col = stamp_col[0, owner, k]
            row = stamp_row[0, owner, k]
            shift = col & (LANES - 1)
            first = (col >> 7) * canvas_rows + row
            back = (LANES - shift) & (LANES - 1)
            halves = []
            for parity in range(2):
                near = reach[pl.ds(first + parity, half, stride=2), :]
                far = reach[pl.ds(first + canvas_rows + parity, half, stride=2), :]
                halves.append(jnp.where(lane_row >= shift, near, far))
            even = pltpu.roll(halves[0], back, 1)
            odd = pltpu.roll(halves[1], (LANES + size - shift) & (LANES - 1), 1)
            stamps[pl.ds(owner * capacity + k, half, stride=slot_pitch), :] = jnp.where(
                lane_half, even, odd
            )
            return inner_carry

        return lax.fori_loop(0, capacity, pick, carry, unroll=capacity)

    lax.fori_loop(0, n_sky, pick_owner, 0)
    for pair in range(pairs):
        windows[:, pair * LANES : (pair + 1) * LANES] = stamps[
            pl.ds(pair * slot_pitch, slots), :
        ].astype(jnp.bfloat16)
    both = wide_dot(windows[...], rendered[...], (((1,), (1,)), ((), ())))
    slot_grad[...] = jnp.where(live > 0, both[:, :n_par] + both[:, n_par:], 0.0)

    def part_copy(step, cross):
        owner = wrapped(me_s + step, n_sky)
        core = 1 - me_core if cross else me_core
        start = pl.multiple_of(owner * capacity + core * per, per)
        return pltpu.make_async_remote_copy(
            src_ref=slot_grad.at[pl.ds(start, per)],
            dst_ref=part_in.at[me_s, me_core],
            send_sem=part_send.at[step, cross],
            recv_sem=part_recv.at[step, cross],
            device_id=(owner, sibling if cross else me_e),
            device_id_type=MESH,
        )

    parts = [(step, cross) for step in range(n_sky) for cross in range(2)][1:]
    for part in parts:
        part_copy(*part).start()
    start = pl.multiple_of(me_s * capacity + me_core * per, per)
    part_in[me_s, me_core] = slot_grad[pl.ds(start, per), :]
    for part in parts:
        part_copy(*part).wait_recv()
    both_cores = (part_in[:, 0] + part_in[:, 1]).reshape(n_sky * per, n_par)
    fold = n_sky * per // 2
    piece[...] = jnp.concatenate([both_cores[:fold], both_cores[fold:]], axis=1)

    def gather_copy(step):
        return pltpu.make_async_remote_copy(
            src_ref=piece,
            dst_ref=gather_in.at[me_e],
            send_sem=gather_send.at[step],
            recv_sem=gather_recv.at[step],
            device_id=(me_s, wrapped(me_e + step, n_epoch)),
            device_id_type=MESH,
        )

    for step in range(1, n_epoch):
        gather_copy(step).start()
    gather_in[me_e] = piece[...]
    for part in parts:
        part_copy(*part).wait_send()
    for step in range(1, n_epoch):
        gather_copy(step).wait()
    summed = []
    for core in range(2):
        total = gather_in[core]
        for chip in range(1, n_epoch // 2):
            total = total + gather_in[2 * chip + core]
        summed.extend([total[:, :n_par], total[:, n_par:]])
    back = jnp.concatenate(summed, axis=0)
    table = jnp.concatenate(
        [
            rows_of[(tile * capacity + core * per + base) // 8]
            for core in range(2)
            for tile in range(n_sky)
            for base in range(0, per, 8)
        ],
        axis=0,
    )
    high = back.astype(jnp.bfloat16)
    rest = back - high.astype(jnp.float32)
    middle_part, low = split_two(rest)
    exact = table.astype(jnp.bfloat16)
    grad_out[...] = wide_dot(
        jnp.concatenate([high, middle_part, low], axis=0),
        jnp.concatenate([exact, exact, exact], axis=0),
        (((0,), (0,)), ((), ())),
    )


def finish(grad, residual, grad_out, residual_out, sems):
    parts = 4
    rows = residual.shape[1] // parts
    copies = [
        pltpu.make_async_copy(
            residual.at[0, pl.ds(part * rows, rows)],
            residual_out.at[0, pl.ds(part * rows, rows)],
            sems.at[part],
        )
        for part in range(parts)
    ] + [pltpu.make_async_copy(grad, grad_out, sems.at[parts])]
    for copy in copies:
        copy.start()
    for copy in copies:
        copy.wait()


def on_device(
    n_sky,
    n_epoch,
    params,
    basis,
    psf_taps,
    send_index,
    tile_count,
    stamp_row,
    stamp_col,
    observed,
    background,
):
    n_par, pixels = basis.shape
    capacity = send_index.shape[2]
    slots = n_sky * capacity
    tile_rows, width = observed.shape[1:]
    size = 64
    margin = size // 2
    canvas_rows = tile_rows + 2 * margin
    planes = width // LANES
    pairs = pixels // LANES
    per = capacity // 2
    f32, bf16 = jnp.float32, jnp.bfloat16
    vmem = pl.BlockSpec(memory_space=pltpu.VMEM)
    smem = pl.BlockSpec(memory_space=pltpu.SMEM)
    dma = pltpu.SemaphoreType.DMA
    hbm = pl.BlockSpec(memory_space=pltpu.HBM)
    params = params.T
    params, basis, psf_taps, send_index, tile_count, stamp_row, stamp_col = (
        pltpu.with_memory_space_constraint(array, pltpu.HBM)
        for array in (params, basis, psf_taps, send_index, tile_count, stamp_row, stamp_col)
    )
    observed, background = (
        pltpu.with_memory_space_constraint(array, pltpu.HBM) for array in (observed, background)
    )
    param_grad, residual = pl.pallas_call(
        functools.partial(kernel, n_sky, n_epoch),
        out_shape=(
            jax.ShapeDtypeStruct((n_par, params.shape[1]), f32),
            jax.ShapeDtypeStruct(observed.shape, f32),
        ),
        in_specs=[vmem, hbm, smem, vmem, smem, smem, smem, smem, hbm, hbm],
        out_specs=(vmem, vmem),
        scratch_shapes=[
            pltpu.VMEM((n_sky, capacity, n_par), bf16),
            pltpu.VMEM((n_sky, capacity, n_par), bf16),
            pltpu.VMEM((2, margin, width), f32),
            pltpu.VMEM((2, margin, width), f32),
            pltpu.VMEM((n_par, pixels), bf16),
            pltpu.VMEM((tile_rows, width), f32),
            pltpu.VMEM((tile_rows, width), f32),
            pltpu.VMEM((pairs * (n_par + 8), LANES), f32),
            pltpu.VMEM((size, pixels), bf16),
            pltpu.VMEM((pairs * (n_par + 8), LANES), f32),
            pltpu.VMEM((2 * n_par, pixels), bf16),
            pltpu.VMEM((pairs * (slots + 8), LANES), f32),
            pltpu.VMEM((canvas_rows, slots * size), bf16),
            pltpu.VMEM((slots * size, width), bf16),
            pltpu.VMEM((4 * margin, width), f32),
            pltpu.VMEM((tile_rows - 2 * margin, width), f32),
            pltpu.VMEM((2, 2 * margin, width), f32),
            pltpu.VMEM(((planes + 1) * canvas_rows, LANES), f32),
            pltpu.VMEM((slots, pixels), bf16),
            pltpu.VMEM((slots, n_par), f32),
            pltpu.VMEM((n_sky, 2, per, n_par), f32),
            pltpu.VMEM((n_sky * per // 2, 2 * n_par), f32),
            pltpu.VMEM((n_epoch, n_sky * per // 2, 2 * n_par), f32),
            dma((6,)),
            dma((n_sky,)),
            dma((n_sky,)),
            dma((2, 2)),
            dma((2, 2)),
            dma((2,)),
            dma((2,)),
            dma((n_sky, 2)),
            dma((n_sky, 2)),
            dma((n_epoch,)),
            dma((n_epoch,)),
        ],
        compiler_params=pltpu.CompilerParams(
            collective_id=0, has_side_effects=True, vmem_limit_bytes=(14 * 1024 + slots * 160) * 1024
        ),
    )(
        params,
        basis,
        psf_taps,
        psf_taps,
        send_index,
        tile_count,
        stamp_row,
        stamp_col,
        observed,
        background,
    )
    param_grad, residual = pl.pallas_call(
        finish,
        out_shape=(
            jax.ShapeDtypeStruct(param_grad.shape, f32),
            jax.ShapeDtypeStruct(residual.shape, f32),
        ),
        in_specs=[vmem, vmem],
        out_specs=(hbm, hbm),
        scratch_shapes=[dma((5,))],
        compiler_params=pltpu.CompilerParams(vmem_limit_bytes=2 * 1024 * 1024),
    )(param_grad, residual)
    return param_grad.T, residual


def solution(mesh):
    in_specs = (
        P("sky", None),
        P(),
        P("epoch", None, None),
        P("sky", None, None),
        P("sky", None),
        P("sky", None, None),
        P("sky", None, None),
        P("epoch", "sky", None),
        P("epoch", "sky", None),
    )
    out_specs = (P("sky", None), P("epoch", "sky", None))
    return jax.shard_map(
        functools.partial(on_device, mesh.shape["sky"], mesh.shape["epoch"]),
        mesh=mesh,
        in_specs=in_specs,
        out_specs=out_specs,
        check_vma=False,
    )
```

```python
import functools

import jax
import jax.numpy as jnp
from jax import lax
from jax.experimental import pallas as pl
from jax.experimental.pallas import tpu as pltpu
from jax.sharding import PartitionSpec as P

MESH = pl.DeviceIdType.MESH
LANES = 128


def split_two(value):
    high = value.astype(jnp.bfloat16)
    return high, (value - high.astype(jnp.float32)).astype(jnp.bfloat16)


def wrapped(value, count):
    return jnp.where(value >= count, value - count, value)


def wide_dot(left, right, dims=(((1,), (0,)), ((), ()))):
    return lax.dot_general(left, right, dims, preferred_element_type=jnp.float32)


def kernel(
    n_sky,
    n_epoch,
    params,
    basis,
    taps_scalar,
    taps_vector,
    send_index,
    tile_count,
    stamp_row,
    stamp_col,
    observed,
    background,
    grad_out,
    residual_out,
    outgoing,
    incoming,
    observed_halo,
    background_halo,
    basis_here,
    observed_here,
    background_here,
    basis_rows,
    basis_mixed,
    rendered_rows,
    rendered,
    rendered_turned,
    stamps,
    row_one,
    moved,
    edges,
    middle,
    light_halo,
    reach,
    windows,
    slot_grad,
    part_in,
    piece,
    gather_in,
    load_sem,
    param_send,
    param_recv,
    halo_send,
    halo_recv,
    light_send,
    light_recv,
    part_send,
    part_recv,
    gather_send,
    gather_recv,
):
    me_s = lax.axis_index("sky")
    me_e = lax.axis_index("epoch")
    n_par, n_source = params.shape
    size = 64
    half = size // 2
    capacity = send_index.shape[2]
    slots = n_sky * capacity
    tile_rows = observed.shape[1]
    width = observed.shape[2]
    margin = half
    canvas_rows = tile_rows + 2 * margin
    planes = width // LANES
    pairs = size * size // LANES
    per = capacity // 2
    n_taps = taps_vector.shape[2]
    reach_taps = (n_taps - 1) // 2
    me_core = lax.rem(me_e, 2)
    sibling = me_e + 1 - 2 * me_core
    slot_pitch = slots + 8
    par_pitch = n_par + 8
    has_above = me_s > 0
    has_below = me_s < n_sky - 1

    loads = [
        pltpu.make_async_copy(
            basis.at[pl.ds(part * (n_par // 4), n_par // 4)],
            basis_here.at[pl.ds(part * (n_par // 4), n_par // 4)],
            load_sem.at[part],
        )
        for part in range(4)
    ] + [
        pltpu.make_async_copy(observed.at[0], observed_here, load_sem.at[4]),
        pltpu.make_async_copy(background.at[0], background_here, load_sem.at[5]),
    ]
    for load in loads:
        load.start()

    barrier = pltpu.get_barrier_semaphore()
    for step in range(n_sky):
        for other in (me_e, sibling)[int(step == 0) :]:
            pl.semaphore_signal(
                barrier, 1, device_id=(wrapped(me_s + step, n_sky), other), device_id_type=MESH
            )
    for step in range(2, n_epoch):
        pl.semaphore_signal(
            barrier,
            1,
            device_id=(me_s, wrapped(me_e - me_core + step, n_epoch)),
            device_id_type=MESH,
        )

    slot_at = lax.broadcasted_iota(jnp.int32, (8, n_source), 0)
    source_at = lax.broadcasted_iota(jnp.int32, (8, n_source), 1)
    rows_of = []
    for base in range(0, slots, 8):
        named = jnp.zeros_like(slot_at)
        for inner in range(8):
            tile, k = divmod(base + inner, capacity)
            named = jnp.where(slot_at == inner, send_index[0, tile, k], named)
        rows_of.append(jnp.where(named == source_at, 1.0, 0.0))
    table = jnp.concatenate(rows_of, axis=0)
    picked = wide_dot(
        table.astype(jnp.bfloat16), params[...], (((1,), (1,)), ((), ()))
    ).astype(jnp.bfloat16)
    for tile in range(n_sky):
        outgoing[tile] = picked[tile * capacity : (tile + 1) * capacity]
    incoming[me_s] = outgoing[me_s]

    def param_copy(step):
        other = wrapped(me_s + step, n_sky)
        return pltpu.make_async_remote_copy(
            src_ref=outgoing.at[other],
            dst_ref=incoming.at[me_s],
            send_sem=param_send.at[step],
            recv_sem=param_recv.at[step],
            device_id=(other, me_e),
            device_id_type=MESH,
        )

    def halo_copies(upward):
        other = me_s - 1 if upward else me_s + 1
        start = 0 if upward else tile_rows - margin
        slot = 1 if upward else 0
        return [
            pltpu.make_async_remote_copy(
                src_ref=array.at[0, pl.ds(start, margin)],
                dst_ref=landing.at[slot],
                send_sem=halo_send.at[which, slot],
                recv_sem=halo_recv.at[which, slot],
                device_id=(other, me_e),
                device_id_type=MESH,
            )
            for which, (array, landing) in enumerate(
                ((observed, observed_halo), (background, background_halo))
            )
        ]

    def light_copies(upward):
        other = me_s - 1 if upward else me_s + 1
        start = 0 if upward else 2 * margin
        slot = 1 if upward else 0
        return [
            pltpu.make_async_remote_copy(
                src_ref=edges.at[pl.ds(start + part * margin, margin)],
                dst_ref=light_halo.at[slot, pl.ds(part * margin, margin)],
                send_sem=light_send.at[slot, part],
                recv_sem=light_recv.at[slot, part],
                device_id=(other, me_e),
                device_id_type=MESH,
            )
            for part in range(2)
        ]

    @pl.when(jnp.logical_not(has_above))
    def _():
        light_halo[0] = jnp.zeros(light_halo.shape[1:], jnp.float32)
        observed_halo[0] = jnp.zeros(observed_halo.shape[1:], jnp.float32)
        background_halo[0] = jnp.ones(background_halo.shape[1:], jnp.float32)

    @pl.when(jnp.logical_not(has_below))
    def _():
        light_halo[1] = jnp.zeros(light_halo.shape[1:], jnp.float32)
        observed_halo[1] = jnp.zeros(observed_halo.shape[1:], jnp.float32)
        background_halo[1] = jnp.ones(background_halo.shape[1:], jnp.float32)

    def natural(value):
        return 2 * (value & (half - 1)) + (value >> 5)

    row_a = natural(lax.broadcasted_iota(jnp.int32, (size, size), 0))
    row_b = natural(lax.broadcasted_iota(jnp.int32, (size, size), 1))
    row_where = row_a - row_b + reach_taps
    col_c = lax.broadcasted_iota(jnp.int32, (size, size), 0)
    col_d = lax.broadcasted_iota(jnp.int32, (size, size), 1)
    col_where = col_d - col_c + reach_taps

    def tap_step(tap, both):
        row_k, col_k = both
        return (
            jnp.where(row_where == tap, taps_scalar[0, 0, tap], row_k),
            jnp.where(col_where == tap, taps_scalar[0, 1, tap], col_k),
        )

    row_k, col_k = lax.fori_loop(
        0,
        n_taps,
        tap_step,
        (jnp.zeros((size, size), jnp.float32), jnp.zeros((size, size), jnp.float32)),
        unroll=17 if n_taps % 17 == 0 else 1,
    )
    total = jnp.sum(taps_vector[0], axis=1, keepdims=True)
    row_high, row_low = split_two(row_k / total[0:1])
    col_k = col_k / total[1:2]
    blank = jnp.zeros_like(col_k)
    col_k = jnp.concatenate(
        [jnp.concatenate([col_k, blank], axis=1), jnp.concatenate([blank, col_k], axis=1)], axis=0
    )
    col_high, col_low = split_two(col_k)
    row_both = jnp.concatenate([row_high, row_low], axis=0)
    col_both = jnp.concatenate(
        [
            jnp.concatenate([col_high, col_low], axis=1),
            jnp.concatenate([col_high, jnp.zeros_like(col_low)], axis=1),
        ],
        axis=0,
    )

    pl.semaphore_wait(barrier, (2 * n_sky - 1) + (n_epoch - 2))
    for step in range(1, n_sky):
        param_copy(step).start()

    @pl.when(has_above)
    def _():
        for copy in halo_copies(True):
            copy.start()

    @pl.when(has_below)
    def _():
        for copy in halo_copies(False):
            copy.start()

    for load in loads[:4]:
        load.wait()
    lane_half = lax.broadcasted_iota(jnp.int32, (half, LANES), 1) < size
    for pair in range(pairs):
        basis_rows[pl.ds(pair * par_pitch, n_par), :] = basis_here[
            :, pair * LANES : (pair + 1) * LANES
        ].astype(jnp.float32)

    def swapped(one, two):
        return (
            jnp.where(lane_half, one, pltpu.roll(two, size, 1)),
            jnp.where(lane_half, pltpu.roll(one, size, 1), two),
        )

    group = 8

    for index in range(n_par // 2 // group):
        for inner in range(group):
            pp = index * group + inner
            one = basis_rows[pl.ds(2 * pp, half, stride=par_pitch), :]
            two = basis_rows[pl.ds(2 * pp + 1, half, stride=par_pitch), :]
            first, second = swapped(one, two)
            basis_mixed[:half, pp * LANES : (pp + 1) * LANES] = first.astype(jnp.bfloat16)
            basis_mixed[half:, pp * LANES : (pp + 1) * LANES] = second.astype(jnp.bfloat16)
    for index in range(n_par // 2 // group):
        by_row = wide_dot(
            row_both, basis_mixed[:, index * group * LANES : (index + 1) * group * LANES]
        )
        by_row = by_row[:size] + by_row[size:]
        tall = jnp.concatenate(
            [by_row[:, inner * LANES : (inner + 1) * LANES] for inner in range(group)], axis=0
        )
        high, low = split_two(tall)
        done = wide_dot(jnp.concatenate([high, low], axis=1), col_both)
        done = done[:, :LANES] + done[:, LANES:]
        for inner in range(group):
            pp = index * group + inner
            base = inner * size
            first, second = swapped(done[base : base + half], done[base + half : base + size])
            rendered_rows[pl.ds(2 * pp, half, stride=par_pitch), :] = first
            rendered_rows[pl.ds(2 * pp + 1, half, stride=par_pitch), :] = second
    for pair in range(pairs):
        high, low = split_two(rendered_rows[pl.ds(pair * par_pitch, n_par), :])
        rendered[:n_par, pair * LANES : (pair + 1) * LANES] = high
        rendered[n_par:, pair * LANES : (pair + 1) * LANES] = low

    for step in range(1, n_sky):
        copy = param_copy(step)
        copy.wait()
    par_slot = lax.broadcasted_iota(jnp.int32, (slots, n_par), 0)
    live = jnp.zeros((slots, n_par), jnp.float32)
    for owner in range(n_sky):
        inside = (par_slot >= owner * capacity) & (
            par_slot < owner * capacity + tile_count[0, owner]
        )
        live = jnp.where(inside & (par_slot < (owner + 1) * capacity), 1.0, live)
    here = incoming[...].reshape(slots, n_par).astype(jnp.float32)
    here = jnp.where(live > 0, here, 0.0)
    here = jnp.concatenate([here, here], axis=1).astype(jnp.bfloat16)
    wide = 8
    for block in range(pairs // wide):
        lanes = slice(block * wide * LANES, (block + 1) * wide * LANES)
        made = wide_dot(here, rendered[:, lanes])
        for inner in range(wide):
            stamps[pl.ds((block * wide + inner) * slot_pitch, slots), :] = made[
                :, inner * LANES : (inner + 1) * LANES
            ]

    lane_row = lax.broadcasted_iota(jnp.int32, (1, LANES), 1)
    level = lax.broadcasted_iota(jnp.int32, (canvas_rows, LANES), 0)
    level = jnp.where(
        level < 2 * margin,
        level,
        jnp.where(level < 4 * margin, level + (canvas_rows - 4 * margin), level - 2 * margin),
    )
    offset = level - natural(lane_row & (size - 1))
    offset = jnp.where(offset < 0, -1, jnp.where(offset > tile_rows, 2 * tile_rows, offset))
    offset = offset.astype(jnp.float32).astype(jnp.bfloat16)
    edge_offset = offset[: 4 * margin]
    core_offset = offset[4 * margin :]
    span = capacity * size

    def target_rows(rows):
        target = jnp.where(lane_row < size, rows[0], rows[1])
        return target.astype(jnp.float32).astype(jnp.bfloat16)

    def place_owner(owner, carry):
        base = pl.multiple_of(owner * span, span)
        for pair in range(capacity // 2):
            rows = []
            for which in range(2):
                k = 2 * pair + which
                col = stamp_col[0, owner, k]
                rows.append(stamp_row[0, owner, k])
                stamp = stamps[pl.ds(owner * capacity + k, half, stride=slot_pitch), :]
                even = pltpu.roll(stamp, col & (LANES - 1), 1)
                odd = pltpu.roll(even, size, 1).astype(jnp.bfloat16)
                even = even.astype(jnp.bfloat16)
                for plane in range(planes):
                    at = lane_row + (plane * LANES) - col
                    inside = jnp.where((at >= 0) & (at < size), 1.0, 0.0).astype(jnp.bfloat16)
                    for parity, data in enumerate((even, odd)):
                        moved[
                            pl.ds(base + k * size + parity * half, half),
                            plane * LANES : (plane + 1) * LANES,
                        ] = data * inside
            target = target_rows(rows)
            row_one[: 4 * margin, pl.ds(base + pair * LANES, LANES)] = jnp.where(
                edge_offset == target, jnp.ones_like(edge_offset), jnp.zeros_like(edge_offset)
            )
        return carry

    lax.fori_loop(0, n_sky, place_owner, 0)
    run = 2 * span if n_sky % 2 == 0 else span

    def gathered(rows):
        def add(index, sum_so_far):
            depth = pl.ds(pl.multiple_of(index * run, run), run)
            return sum_so_far + wide_dot(row_one[rows, depth], moved[depth, :])

        first = wide_dot(row_one[rows, :run], moved[:run, :])
        return lax.fori_loop(1, n_sky * span // run, add, first)

    edges[...] = gathered(slice(0, 4 * margin))

    @pl.when(has_above)
    def _():
        for copy in light_copies(True):
            copy.start()

    @pl.when(has_below)
    def _():
        for copy in light_copies(False):
            copy.start()

    def residual_of(image, seen, sky):
        decay = jnp.exp(-jnp.abs(image))
        model = sky + (jnp.maximum(image, 0.0) + jnp.log(1.0 + decay))
        numerator = jnp.where(image >= 0, 1.0, decay)
        return (seen - model) * numerator / (model * (1.0 + decay))

    def keep(value, start):
        rounded = value.astype(jnp.bfloat16).astype(jnp.float32)
        for plane in range(planes):
            reach[pl.ds(plane * canvas_rows + start, margin), :] = rounded[
                :, plane * LANES : (plane + 1) * LANES
            ]

    def middle_owner(owner, carry):
        base = pl.multiple_of(owner * span, span)
        for pair in range(capacity // 2):
            target = target_rows([stamp_row[0, owner, 2 * pair + which] for which in range(2)])
            row_one[4 * margin :, pl.ds(base + pair * LANES, LANES)] = jnp.where(
                core_offset == target, jnp.ones_like(core_offset), jnp.zeros_like(core_offset)
            )
        return carry

    lax.fori_loop(0, n_sky, middle_owner, 0)
    middle[...] = gathered(slice(4 * margin, canvas_rows))
    for load in loads[4:]:
        load.wait()

    def core_chunk(index, carry):
        start = pl.multiple_of(index * margin, margin)
        inner = pl.multiple_of(start + margin, margin)
        value = residual_of(
            middle[pl.ds(start, margin), :],
            observed_here[pl.ds(inner, margin), :],
            background_here[pl.ds(inner, margin), :],
        )
        residual_out[0, pl.ds(inner, margin), :] = value
        keep(value, pl.multiple_of(start + 2 * margin, margin))
        return carry

    lax.fori_loop(0, canvas_rows // margin - 4, core_chunk, 0, unroll=3)
    reach[planes * canvas_rows :, :] = jnp.zeros((canvas_rows, LANES), jnp.float32)

    for pair in range(pairs):
        rendered_turned[pair * LANES : (pair + 1) * LANES, :] = rendered[
            :, pair * LANES : (pair + 1) * LANES
        ].T

    @pl.when(has_above)
    def _():
        for copy in light_copies(True):
            copy.wait_send()
        for copy in light_copies(False):
            copy.wait_recv()
        for copy in halo_copies(True):
            copy.wait_send()
        for copy in halo_copies(False):
            copy.wait_recv()

    @pl.when(has_below)
    def _():
        for copy in light_copies(False):
            copy.wait_send()
        for copy in light_copies(True):
            copy.wait_recv()
        for copy in halo_copies(False):
            copy.wait_send()
        for copy in halo_copies(True):
            copy.wait_recv()

    for slot, exists in ((0, has_above), (1, has_below)):
        outer = 0 if slot == 0 else canvas_rows - margin
        inner = margin if slot == 0 else canvas_rows - 2 * margin
        outer_light = 0 if slot == 0 else margin
        inner_light = margin - outer_light
        value = residual_of(
            edges[pl.ds(2 * slot * margin + outer_light, margin), :]
            + light_halo[slot, pl.ds(outer_light, margin), :],
            observed_halo[slot],
            background_halo[slot],
        )
        keep(jnp.where(exists, value, 0.0), outer)
        value = residual_of(
            edges[pl.ds(2 * slot * margin + inner_light, margin), :]
            + light_halo[slot, pl.ds(inner_light, margin), :],
            observed_here[pl.ds(inner - margin, margin), :],
            background_here[pl.ds(inner - margin, margin), :],
        )
        residual_out[0, pl.ds(inner - margin, margin), :] = value
        keep(value, inner)

    def pick_owner(owner, carry):
        def pick(k, inner_carry):
            col = stamp_col[0, owner, k]
            row = stamp_row[0, owner, k]
            shift = col & (LANES - 1)
            first = (col >> 7) * canvas_rows + row
            back = (LANES - shift) & (LANES - 1)
            halves = []
            for parity in range(2):
                near = reach[pl.ds(first + parity, half, stride=2), :]
                far = reach[pl.ds(first + canvas_rows + parity, half, stride=2), :]
                halves.append(jnp.where(lane_row >= shift, near, far))
            even = pltpu.roll(halves[0], back, 1)
            odd = pltpu.roll(halves[1], (LANES + size - shift) & (LANES - 1), 1)
            stamps[pl.ds(owner * capacity + k, half, stride=slot_pitch), :] = jnp.where(
                lane_half, even, odd
            )
            return inner_carry

        return lax.fori_loop(0, capacity, pick, carry, unroll=capacity)

    lax.fori_loop(0, n_sky, pick_owner, 0)
    for pair in range(pairs):
        windows[:, pair * LANES : (pair + 1) * LANES] = stamps[
            pl.ds(pair * slot_pitch, slots), :
        ].astype(jnp.bfloat16)
    both = wide_dot(windows[...], rendered_turned[...])
    slot_grad[...] = jnp.where(live > 0, both[:, :n_par] + both[:, n_par:], 0.0)

    def part_copy(step, cross):
        owner = wrapped(me_s + step, n_sky)
        core = 1 - me_core if cross else me_core
        start = pl.multiple_of(owner * capacity + core * per, per)
        return pltpu.make_async_remote_copy(
            src_ref=slot_grad.at[pl.ds(start, per)],
            dst_ref=part_in.at[me_s, me_core],
            send_sem=part_send.at[step, cross],
            recv_sem=part_recv.at[step, cross],
            device_id=(owner, sibling if cross else me_e),
            device_id_type=MESH,
        )

    parts = [(step, cross) for step in range(n_sky) for cross in range(2)][1:]
    for part in parts:
        part_copy(*part).start()
    start = pl.multiple_of(me_s * capacity + me_core * per, per)
    part_in[me_s, me_core] = slot_grad[pl.ds(start, per), :]
    for part in parts:
        part_copy(*part).wait_recv()
    both_cores = (part_in[:, 0] + part_in[:, 1]).reshape(n_sky * per, n_par)
    fold = n_sky * per // 2
    piece[...] = jnp.concatenate([both_cores[:fold], both_cores[fold:]], axis=1)

    def gather_copy(step):
        return pltpu.make_async_remote_copy(
            src_ref=piece,
            dst_ref=gather_in.at[me_e],
            send_sem=gather_send.at[step],
            recv_sem=gather_recv.at[step],
            device_id=(me_s, wrapped(me_e + step, n_epoch)),
            device_id_type=MESH,
        )

    for step in range(1, n_epoch):
        gather_copy(step).start()
    gather_in[me_e] = piece[...]
    for part in parts:
        part_copy(*part).wait_send()
    for step in range(1, n_epoch):
        gather_copy(step).wait()
    summed = []
    for core in range(2):
        total = gather_in[core]
        for chip in range(1, n_epoch // 2):
            total = total + gather_in[2 * chip + core]
        summed.extend([total[:, :n_par], total[:, n_par:]])
    back = jnp.concatenate(summed, axis=0)
    table = jnp.concatenate(
        [
            rows_of[(tile * capacity + core * per + base) // 8]
            for core in range(2)
            for tile in range(n_sky)
            for base in range(0, per, 8)
        ],
        axis=0,
    )
    high = back.astype(jnp.bfloat16)
    rest = back - high.astype(jnp.float32)
    middle_part, low = split_two(rest)
    exact = table.astype(jnp.bfloat16)
    grad_out[...] = wide_dot(
        jnp.concatenate([high, middle_part, low], axis=0),
        jnp.concatenate([exact, exact, exact], axis=0),
        (((0,), (0,)), ((), ())),
    )


def finish(grad, residual, grad_out, residual_out, sems):
    parts = 4
    rows = residual.shape[1] // parts
    copies = [
        pltpu.make_async_copy(
            residual.at[0, pl.ds(part * rows, rows)],
            residual_out.at[0, pl.ds(part * rows, rows)],
            sems.at[part],
        )
        for part in range(parts)
    ] + [pltpu.make_async_copy(grad, grad_out, sems.at[parts])]
    for copy in copies:
        copy.start()
    for copy in copies:
        copy.wait()


def on_device(
    n_sky,
    n_epoch,
    params,
    basis,
    psf_taps,
    send_index,
    tile_count,
    stamp_row,
    stamp_col,
    observed,
    background,
):
    n_par, pixels = basis.shape
    capacity = send_index.shape[2]
    slots = n_sky * capacity
    tile_rows, width = observed.shape[1:]
    size = 64
    margin = size // 2
    canvas_rows = tile_rows + 2 * margin
    planes = width // LANES
    pairs = pixels // LANES
    per = capacity // 2
    f32, bf16 = jnp.float32, jnp.bfloat16
    vmem = pl.BlockSpec(memory_space=pltpu.VMEM)
    smem = pl.BlockSpec(memory_space=pltpu.SMEM)
    dma = pltpu.SemaphoreType.DMA
    hbm = pl.BlockSpec(memory_space=pltpu.HBM)
    params = params.T
    params, basis, psf_taps, send_index, tile_count, stamp_row, stamp_col = (
        pltpu.with_memory_space_constraint(array, pltpu.HBM)
        for array in (params, basis, psf_taps, send_index, tile_count, stamp_row, stamp_col)
    )
    observed, background = (
        pltpu.with_memory_space_constraint(array, pltpu.HBM) for array in (observed, background)
    )
    param_grad, residual = pl.pallas_call(
        functools.partial(kernel, n_sky, n_epoch),
        out_shape=(
            jax.ShapeDtypeStruct((n_par, params.shape[1]), f32),
            jax.ShapeDtypeStruct(observed.shape, f32),
        ),
        in_specs=[vmem, hbm, smem, vmem, smem, smem, smem, smem, hbm, hbm],
        out_specs=(vmem, vmem),
        scratch_shapes=[
            pltpu.VMEM((n_sky, capacity, n_par), bf16),
            pltpu.VMEM((n_sky, capacity, n_par), bf16),
            pltpu.VMEM((2, margin, width), f32),
            pltpu.VMEM((2, margin, width), f32),
            pltpu.VMEM((n_par, pixels), bf16),
            pltpu.VMEM((tile_rows, width), f32),
            pltpu.VMEM((tile_rows, width), f32),
            pltpu.VMEM((pairs * (n_par + 8), LANES), f32),
            pltpu.VMEM((size, pixels), bf16),
            pltpu.VMEM((pairs * (n_par + 8), LANES), f32),
            pltpu.VMEM((2 * n_par, pixels), bf16),
            pltpu.VMEM((pixels, 2 * n_par), bf16),
            pltpu.VMEM((pairs * (slots + 8), LANES), f32),
            pltpu.VMEM((canvas_rows, slots * size), bf16),
            pltpu.VMEM((slots * size, width), bf16),
            pltpu.VMEM((4 * margin, width), f32),
            pltpu.VMEM((tile_rows - 2 * margin, width), f32),
            pltpu.VMEM((2, 2 * margin, width), f32),
            pltpu.VMEM(((planes + 1) * canvas_rows, LANES), f32),
            pltpu.VMEM((slots, pixels), bf16),
            pltpu.VMEM((slots, n_par), f32),
            pltpu.VMEM((n_sky, 2, per, n_par), f32),
            pltpu.VMEM((n_sky * per // 2, 2 * n_par), f32),
            pltpu.VMEM((n_epoch, n_sky * per // 2, 2 * n_par), f32),
            dma((6,)),
            dma((n_sky,)),
            dma((n_sky,)),
            dma((2, 2)),
            dma((2, 2)),
            dma((2, 2)),
            dma((2, 2)),
            dma((n_sky, 2)),
            dma((n_sky, 2)),
            dma((n_epoch,)),
            dma((n_epoch,)),
        ],
        compiler_params=pltpu.CompilerParams(
            collective_id=0, has_side_effects=True, vmem_limit_bytes=(14 * 1024 + slots * 160) * 1024
        ),
    )(
        params,
        basis,
        psf_taps,
        psf_taps,
        send_index,
        tile_count,
        stamp_row,
        stamp_col,
        observed,
        background,
    )
    param_grad, residual = pl.pallas_call(
        finish,
        out_shape=(
            jax.ShapeDtypeStruct(param_grad.shape, f32),
            jax.ShapeDtypeStruct(residual.shape, f32),
        ),
        in_specs=[vmem, vmem],
        out_specs=(hbm, hbm),
        scratch_shapes=[dma((5,))],
        compiler_params=pltpu.CompilerParams(vmem_limit_bytes=2 * 1024 * 1024),
    )(param_grad, residual)
    return param_grad.T, residual


def solution(mesh):
    in_specs = (
        P("sky", None),
        P(),
        P("epoch", None, None),
        P("sky", None, None),
        P("sky", None),
        P("sky", None, None),
        P("sky", None, None),
        P("epoch", "sky", None),
        P("epoch", "sky", None),
    )
    out_specs = (P("sky", None), P("epoch", "sky", None))
    return jax.shard_map(
        functools.partial(on_device, mesh.shape["sky"], mesh.shape["epoch"]),
        mesh=mesh,
        in_specs=in_specs,
        out_specs=out_specs,
        check_vma=False,
    )
```
